512 devices in a mesh: own: 64 (over y, z), rep: 8 (over x, core).
Axes of the slice: x: 4, y: 8, z: 8, core: 2. Of those that a mesh axis runs over, the one named last changes fastest.
Arguments:
- sample_rows: bfloat16 [524288, 768], P(('own', 'rep'))
- destination: int32 [524288], P(('own', 'rep')), may hold values from 0 to 524287, as said below
- neighbours: int32 [524288, 4], P(('own', 'rep')), may hold values from 0 to 2047, as said below
- centroids: bfloat16 [256, 8, 128, 768], P('own', 'rep'), may hold values from -6 to 6
Outputs:
- new_centroids: bfloat16 [256, 8, 128, 768], P('own', 'rep')
- row_cost: float32 [524288], P(('own', 'rep'))
The draws below stay inside these ranges and needn't reach their ends.
Inputs may be any that keep to these rules, and one draw needn't show every extreme that they name: destination is a permutation. Numbering devices own-major (device t = own index * 8 + rep index), ingested row i of device s goes to device t = destination[i] // 1024, and the rows that device t receives from device s fill its positions s * 2 up to (s + 1) * 2 - 1; every device sends exactly 2 rows to every device. `neighbours`: each regrouped row on the device with own index o and rep index r lists 4 different blocks a * 8 + r with a inside the grid and o * 4 - 1 <= a <= o * 4 + 4.
All inputs are finite; a program needn't handle non-finite values.
Results may differ from the reference program's by a relative error of at most 0.0075.
Values may be sent and summed in bfloat16 or wider, within the bound.
No kernel may reach another device: no remote copies, remote signals or barrier semaphores. Data moves between devices by JAX's collectives and lax.ppermute only.
A program may use at most 64 MiB of HBM per device.

```python
import math
import jax
import jax.numpy as jnp
from jax import lax

D = 768
CB = 128
BLK = 4
NB = 4
ITERS = 2
ROWS = 1024
GA = 256
N_OWN = 64
N_REP = 8


def draw_sample_rows(key, part):
    total_rows = ROWS * N_OWN * N_REP
    return jax.random.normal(key, (total_rows, D), jnp.float32).astype(jnp.bfloat16)


def shuffle_rows(single_key):
    return jax.random.permutation(single_key, ROWS)


def draw_destination(key, part):
    sources = N_OWN * N_REP
    per_pair = ROWS // sources
    key_list = jax.random.split(key, sources)
    orders = jax.vmap(shuffle_rows)(key_list).astype(jnp.int32)
    source = jnp.arange(sources, dtype=jnp.int32)[:, None]
    target = orders // per_pair
    slot_index = orders % per_pair
    return (target * ROWS + source * per_pair + slot_index).reshape(sources * ROWS).astype(jnp.int32)


def draw_neighbours(key, part):
    total_rows = ROWS * N_OWN * N_REP
    window = BLK + 2
    position = jnp.arange(total_rows, dtype=jnp.int32)
    device = position // ROWS
    owner_index = device // N_REP
    column = device % N_REP
    first_block = owner_index * BLK - 1
    offsets = jnp.arange(window, dtype=jnp.int32)
    grid_first = first_block[:, None] + offsets[None, :]
    inside = (grid_first >= 0) & (grid_first < BLK * N_OWN)
    scores = jax.random.randint(key, (total_rows, window), 0, 1 << 20, dtype=jnp.int32) * 16 + offsets[None, :]
    scores = jnp.where(inside, scores, -1)
    picked = lax.top_k(scores, NB)[1]
    chosen = jnp.take_along_axis(grid_first, picked, axis=1)
    return (chosen * N_REP + column[:, None]).astype(jnp.int32)


def levels(stream_key, shape, pieces, least, high):
    factor_of = 1.0
    for dim, blocks in pieces:
        heights = jax.random.uniform(jax.random.fold_in(jax.random.fold_in(stream_key, 6), dim), (blocks,), jnp.float32, least / len(pieces), high / len(pieces))
        factor_of = factor_of * jnp.repeat(jnp.exp(heights), shape[dim] // blocks).reshape((-1,) + (1,) * (len(shape) - 1 - dim))
    return factor_of


def bell_draw(key, shape, scale, bound, pieces=(), held_as=jnp.bfloat16):
    values = scale * jax.random.normal(key, shape, jnp.float32)
    if pieces:
        values = values * levels(key, shape, pieces, -0.22, 0.18)
    return jnp.clip(values, -bound, bound).astype(held_as)


def setup_inputs(seed: int = 0) -> dict:
    splits = jax.random.split(jax.random.key(seed), 5)
    sample_rows = draw_sample_rows(jax.random.fold_in(splits[4], 71), 0)
    destination = draw_destination(jax.random.fold_in(splits[4], 71), 0)
    neighbours = draw_neighbours(jax.random.fold_in(splits[4], 71), 0)
    centroids = bell_draw(splits[3], (GA, N_REP, CB, D), 1.0, 6.0, ((0, 64), (1, 8)))
    return {"sample_rows": sample_rows, "destination": destination, "neighbours": neighbours, "centroids": centroids}


PRIOR = 1.0

def soft_assign(local_rows, local_ids, candidates):
    window, per_block, features = candidates.shape
    flat_blocks = candidates.reshape(window * per_block, features)
    inv_scale = 0.5 / math.sqrt(features)
    cross = lax.dot_general(local_rows, flat_blocks, (((1,), (1,)), ((), ())), preferred_element_type=jnp.float32)
    cand_wide = flat_blocks.astype(jnp.float32)
    cand_norm = lax.optimization_barrier(jnp.sum(cand_wide * cand_wide, axis=1))
    rows_wide = local_rows.astype(jnp.float32)
    rows_norm = lax.optimization_barrier(jnp.sum(rows_wide * rows_wide, axis=1))
    logits = (2.0 * cross - rows_norm[:, None] - cand_norm[None, :]) * inv_scale
    logits = logits.reshape(local_rows.shape[0], window, per_block)
    slots = jnp.arange(window, dtype=jnp.int32)
    chosen = jnp.any(local_ids[:, :, None] == slots[None, None, :], axis=1)[:, :, None]
    masked = jnp.where(chosen, logits, -jnp.inf)
    row_top = lax.optimization_barrier(jnp.max(masked, axis=(1, 2), keepdims=True))
    weights = jnp.where(chosen, jnp.exp(masked - row_top), 0.0)
    row_total = lax.optimization_barrier(jnp.sum(weights, axis=(1, 2), keepdims=True))
    responses = weights / row_total
    row_cost = -(row_top[:, 0, 0] + jnp.log(row_total[:, 0, 0]))
    resp_half = responses.reshape(local_rows.shape[0], window * per_block).astype(jnp.bfloat16)
    part_sums = lax.dot_general(resp_half, local_rows, (((0,), (0,)), ((), ())), preferred_element_type=jnp.float32)
    part_counts = lax.optimization_barrier(jnp.sum(responses, axis=0))
    return (part_sums.reshape(window, per_block, features), part_counts, row_cost)

def refresh(total, tally, previous):
    return ((total + PRIOR * previous.astype(jnp.float32)) / (tally[..., None] + PRIOR)).astype(jnp.bfloat16)

def reference(sample_rows, destination, neighbours, centroids):
    regrouped = jnp.zeros_like(sample_rows).at[destination].set(sample_rows)
    row_tiles = regrouped.reshape(N_OWN, N_REP, ROWS, D)
    owners = jnp.arange(N_OWN, dtype=jnp.int32)
    local_ids = (neighbours // N_REP).reshape(N_OWN, N_REP, ROWS, NB) - (owners * BLK - 1)[:, None, None, None]
    local_ids = local_ids.astype(jnp.int32)
    current = centroids.reshape(N_OWN, BLK, N_REP, CB, D)
    row_cost = jnp.zeros((N_OWN, N_REP, ROWS), jnp.float32)
    for iteration in range(ITERS):
        flat_grid = current.reshape(N_OWN * BLK, N_REP, CB, D)
        padded = jnp.pad(flat_grid, ((1, 1), (0, 0), (0, 0), (0, 0)))

        def one_owner(packed):
            tile_rows, tile_ids, owner_index = packed
            window = lax.dynamic_slice_in_dim(padded, owner_index * BLK, BLK + 2, 0)
            window = jnp.moveaxis(window, 1, 0)
            return jax.vmap(soft_assign)(tile_rows, tile_ids, window)
        part_sums, part_counts, row_cost = lax.map(one_owner, (row_tiles, local_ids, owners))
        zero_sums = jnp.zeros_like(part_sums[:1, :, 0])
        zero_counts = jnp.zeros_like(part_counts[:1, :, 0])
        from_left = jnp.concatenate([zero_sums, part_sums[:-1, :, BLK + 1]], axis=0)
        from_right = jnp.concatenate([part_sums[1:, :, 0], zero_sums], axis=0)
        total = part_sums[:, :, 1:BLK + 1].at[:, :, 0].add(from_left).at[:, :, BLK - 1].add(from_right)
        left_counts = jnp.concatenate([zero_counts, part_counts[:-1, :, BLK + 1]], axis=0)
        right_counts = jnp.concatenate([part_counts[1:, :, 0], zero_counts], axis=0)
        tally = part_counts[:, :, 1:BLK + 1].at[:, :, 0].add(left_counts).at[:, :, BLK - 1].add(right_counts)
        previous = jnp.moveaxis(current, 2, 1)
        fresh = refresh(total, tally, previous)
        current = jnp.moveaxis(fresh, 1, 2)
    return (current.reshape(N_OWN * BLK, N_REP, CB, D), row_cost.reshape(N_OWN * N_REP * ROWS))
```

```python
import functools
import math

import jax
import jax.numpy as jnp
from jax import lax
from jax.experimental import pallas as pl
from jax.experimental.pallas import tpu as pltpu
from jax.sharding import PartitionSpec as P

PRIOR = 1.0
LOG2E = 1.4426950408889634
LANES = 128
MASS_ROWS = 16
VMEM = pl.BlockSpec(memory_space=pltpu.VMEM)
F32 = jnp.float32
BF16 = jnp.bfloat16


def call(kernel, outs, scratch=(), flops=0, limit=24):
    return pl.pallas_call(
        kernel,
        out_shape=outs,
        out_specs=jax.tree.map(lambda _: VMEM, outs),
        scratch_shapes=list(scratch),
        compiler_params=pltpu.CompilerParams(vmem_limit_bytes=limit << 20),
        cost_estimate=pl.CostEstimate(flops=flops, bytes_accessed=1 << 20, transcendentals=0),
    )


def sds(shape, dtype):
    return jax.ShapeDtypeStruct(shape, dtype)


def matmul(a, b, contract):
    return lax.dot_general(a, b, (contract, ((), ())), preferred_element_type=F32)


def regroup_kernel(pairs, dest_ref, rows_ref, out_ref, wide):
    count, features = rows_ref.shape
    per_pair = count // pairs
    chunks = features // LANES
    dest = dest_ref[...]
    place = lax.rem(dest, per_pair) * pairs + lax.div(dest, count)
    rows = rows_ref[...]
    step = 256
    for start in range(0, count, step):
        ids = lax.broadcasted_iota(jnp.int32, (step, count), 0) + start
        pick = jnp.where(ids == place, 1.0, 0.0).astype(BF16)
        moved = matmul(pick, rows, ((1,), (0,)))
        slot, first = divmod(start, pairs)
        for f in range(chunks):
            line = (first * chunks + f) * per_pair + slot
            wide[pl.ds(line, step, stride=chunks * per_pair), :] = moved[:, f * LANES : (f + 1) * LANES]
    lines = count * chunks
    for start in range(0, lines, 512):
        out_ref[pl.ds(start, 512), :] = wide[pl.ds(start, 512), :].astype(BF16)


def unpack_rows(lines_ref, rows_ref, wide, pairs):
    count, features = rows_ref.shape
    per_pair = count // pairs
    chunks = features // LANES
    for start in range(0, count * chunks, 512):
        wide[pl.ds(start, 512), :] = lines_ref[pl.ds(start, 512), :].astype(F32)
    for slot in range(per_pair):
        for f in range(chunks):
            part = wide[pl.ds(f * per_pair + slot, pairs, stride=chunks * per_pair), :]
            rows_ref[pl.ds(slot * pairs, pairs), f * LANES : (f + 1) * LANES] = part.astype(BF16)


def assign(rows_ref, ids_ref, blocks, resp_ref, tops_ref=None):
    count, features = rows_ref.shape
    window = len(blocks)
    half = 0.5 * LOG2E / math.sqrt(features)
    bias = []
    for block in blocks:
        wide = block.astype(F32)
        bias.append(jnp.sum(wide * wide, axis=1, keepdims=True) * half)
    flat = jnp.concatenate(blocks, axis=0)
    per_block = blocks[0].shape[0]
    mass = [0.0] * window
    step = 256
    for start in range(0, count, step):
        rows = rows_ref[pl.ds(start, step), :]
        ids = ids_ref[:, start : start + step]
        cross = matmul(flat, rows, ((1,), (1,)))
        scores = []
        top = None
        for w in range(window):
            hit = jnp.max(jnp.where(ids == w, 0.0, -jnp.inf), axis=0, keepdims=True)
            score = cross[w * per_block : (w + 1) * per_block] * (2.0 * half) - bias[w] + hit
            scores.append(score)
            here = jnp.max(score, axis=0, keepdims=True)
            top = here if top is None else jnp.maximum(top, here)
        total = None
        for w in range(window):
            scores[w] = jnp.exp2(scores[w] - top)
            here = jnp.sum(scores[w], axis=0, keepdims=True)
            total = here if total is None else total + here
        scale = 1.0 / total
        for w in range(window):
            resp = scores[w] * scale
            resp_ref[w * per_block : (w + 1) * per_block, start : start + step] = resp.astype(BF16)
            mass[w] = mass[w] + resp
        if tops_ref is not None:
            tops_ref[:, start : start + step] = top * (1.0 / LOG2E) + jnp.log(total)
    return [jnp.sum(m, axis=1, keepdims=True) for m in mass]


def diagonal(size):
    across = lax.broadcasted_iota(jnp.int32, (size, size), 0)
    return across == lax.broadcasted_iota(jnp.int32, (size, size), 1)


def pack_mass(masses):
    size = masses[0].shape[0]
    eye = diagonal(size)
    lines = [jnp.sum(jnp.where(eye, m, 0.0), axis=0, keepdims=True) for m in masses]
    line = jnp.concatenate(lines, axis=1)
    high = line.astype(BF16).astype(F32)
    row = lax.broadcasted_iota(jnp.int32, (MASS_ROWS, line.shape[1]), 0)
    return jnp.where(row == 0, high, jnp.where(row == 1, line - high, 0.0)).astype(BF16)


def unpack_mass(packed, which, size):
    line = packed[:, which * size : (which + 1) * size].astype(F32)
    line = jnp.sum(line, axis=0, keepdims=True)
    return jnp.sum(jnp.where(diagonal(size), line, 0.0), axis=1, keepdims=True)


def package(pkg_ref, sums, masses):
    size = masses[0].shape[0]
    blocks = len(sums)
    for k in range(blocks):
        pkg_ref[k * size : (k + 1) * size, :] = sums[k].astype(BF16)
    packed = pack_mass(masses)
    pkg_ref[blocks * size :, : blocks * size] = packed
    rest = pkg_ref.shape[1] - blocks * size
    pkg_ref[blocks * size :, blocks * size :] = jnp.zeros((MASS_ROWS, rest), BF16)


def refresh(total, tally, previous):
    return ((total + PRIOR * previous.astype(F32)) / (tally + PRIOR)).astype(BF16)


def window_blocks(left_ref, own_ref, right_ref):
    return [left_ref[...]] + [own_ref[k] for k in range(own_ref.shape[0])] + [right_ref[...]]


def first_kernel(
    pairs, lines_ref, ids_ref, left_ref, own_ref, right_ref,
    rows_ref, resp_ref, sums_ref, mass_ref, up_ref, down_ref, wide,
):
    unpack_rows(lines_ref, rows_ref, wide, pairs)
    blocks = window_blocks(left_ref, own_ref, right_ref)
    mass = assign(rows_ref, ids_ref, blocks, resp_ref)
    size = own_ref.shape[1]
    last = len(blocks) - 1
    rows = rows_ref[...]
    sums = {}
    for w in (0, 1, last - 1, last):
        sums[w] = matmul(resp_ref[w * size : (w + 1) * size, :], rows, ((1,), (0,)))
        sums_ref[w] = sums[w]
    for w in range(last + 1):
        mass_ref[w * size : (w + 1) * size, :] = mass[w]
    package(up_ref, [sums[last - 1], sums[last]], [mass[last - 1], mass[last]])
    package(down_ref, [sums[0], sums[1]], [mass[0], mass[1]])


def inner_kernel(rows_ref, resp_ref, mass_ref, own_ref, fresh_ref, norm_ref):
    blocks, size, _ = own_ref.shape
    rows = rows_ref[...]
    for k in range(1, blocks - 1):
        w = k + 1
        total = matmul(resp_ref[w * size : (w + 1) * size, :], rows, ((1,), (0,)))
        fresh_ref[k - 1] = refresh(total, mass_ref[w * size : (w + 1) * size, :], own_ref[k])
    eye = diagonal(LANES)
    for start in range(0, rows_ref.shape[0], LANES):
        wide = rows_ref[pl.ds(start, LANES), :].astype(F32)
        norm = jnp.sum(wide * wide, axis=1, keepdims=True)
        norm_ref[:, start : start + LANES] = jnp.sum(jnp.where(eye, norm, 0.0), axis=0, keepdims=True)


def second_kernel(
    rows_ref, ids_ref, left_ref, own_ref, right_ref, sums_ref, mass_ref, fresh_ref, norm_ref, below_ref, above_ref,
    edge_ref, resp_ref, mass_out, cost_ref, up_ref, down_ref,
):
    count, size, _ = own_ref.shape
    last = count + 1
    old = {0: left_ref[...], 1: own_ref[0], last - 1: own_ref[count - 1], last: right_ref[...]}
    new = {}
    for pkg, ws in ((below_ref, (0, 1)), (above_ref, (last - 1, last))):
        packed = pkg[2 * size :, : 2 * size]
        for k, w in enumerate(ws):
            total = sums_ref[w] + pkg[k * size : (k + 1) * size, :].astype(F32)
            tally = mass_ref[w * size : (w + 1) * size, :] + unpack_mass(packed, k, size)
            new[w] = refresh(total, tally, old[w])
    edge_ref[0] = new[1]
    edge_ref[1] = new[last - 1]
    blocks = [new[0], new[1]] + [fresh_ref[k] for k in range(count - 2)] + [new[last - 1], new[last]]
    mass = assign(rows_ref, ids_ref, blocks, resp_ref, cost_ref)
    half = 0.5 / math.sqrt(rows_ref.shape[1])
    cost_ref[...] = norm_ref[...] * half - cost_ref[...]
    for w in range(last + 1):
        mass_out[w * size : (w + 1) * size, :] = mass[w]
    rows = rows_ref[...]
    for pkg, w in ((up_ref, last), (down_ref, 0)):
        total = matmul(resp_ref[w * size : (w + 1) * size, :], rows, ((1,), (0,)))
        package(pkg, [total], [mass[w]])


def own_kernel(rows_ref, resp_ref, mass_ref, edge_ref, fresh_ref, done_ref, part_ref):
    blocks, size, _ = part_ref.shape[0] + fresh_ref.shape[0], part_ref.shape[1], None
    rows = rows_ref[...]
    for k in range(blocks):
        w = k + 1
        total = matmul(resp_ref[w * size : (w + 1) * size, :], rows, ((1,), (0,)))
        if 0 < k < blocks - 1:
            done_ref[k - 1] = refresh(total, mass_ref[w * size : (w + 1) * size, :], fresh_ref[k - 1])
        else:
            part_ref[0 if k == 0 else 1] = total


def last_kernel(done_ref, part_ref, mass_ref, edge_ref, below_ref, above_ref, out_ref):
    blocks, size, _ = out_ref.shape
    for k in range(1, blocks - 1):
        out_ref[k] = done_ref[k - 1]
    for e, (k, pkg) in enumerate(((0, below_ref), (blocks - 1, above_ref))):
        w = k + 1
        total = part_ref[e] + pkg[:size, :].astype(F32)
        tally = mass_ref[w * size : (w + 1) * size, :] + unpack_mass(pkg[size:, :size], 0, size)
        out_ref[k] = refresh(total, tally, edge_ref[e])


def swap(up, down, axis):
    devices = lax.axis_size(axis)
    pairs = [(i, i + 1) for i in range(devices - 1)]
    below = lax.ppermute(up, axis, pairs)
    above = lax.ppermute(down, axis, [(j, i) for i, j in pairs])
    return below, above


def per_device(sample_rows, destination, neighbours, centroids):
    own_count, rep_count = lax.axis_size("own"), lax.axis_size("rep")
    pairs = own_count * rep_count
    count, features = sample_rows.shape
    per_pair = count // pairs
    chunks = features // LANES
    lines = count * chunks
    blocks, _, size, _ = centroids.shape
    window = blocks + 2
    own = centroids.reshape(blocks, size, features)
    wide = pltpu.VMEM((lines + chunks * per_pair + 4, LANES), F32)
    dot = 2 * count * features

    outgoing = call(
        functools.partial(regroup_kernel, pairs), sds((lines, LANES), BF16), [wide], dot * count
    )(destination.reshape(1, count), sample_rows)
    left, right = swap(own[blocks - 1], own[0], "own")
    first_block = lax.axis_index("own") * blocks - 1
    ids = (neighbours // rep_count - first_block).T
    ids = ids.reshape(-1, pairs, per_pair).swapaxes(1, 2).reshape(-1, count)
    arrived = lax.all_to_all(
        outgoing.reshape(pairs, lines // pairs // 4, 4, LANES), ("own", "rep"), split_axis=0, concat_axis=0, tiled=True
    ).reshape(lines, LANES)

    resp = sds((window * size, count), BF16)
    mass = sds((window * size, 1), F32)
    two = sds((2 * size + MASS_ROWS, features), BF16)
    one = sds((size + MASS_ROWS, features), BF16)
    inner = sds((blocks - 2, size, features), BF16)
    rows, resp1, sums1, mass1, up1, down1 = call(
        functools.partial(first_kernel, pairs),
        (sds((count, features), BF16), resp, sds((window, size, features), F32), mass, two, two),
        [wide],
        dot * (window + 4) * size,
    )(arrived, ids, left, own, right)
    below1, above1 = swap(up1, down1, "own")
    fresh, norm = call(inner_kernel, (inner, sds((1, count), F32)), (), dot * 2 * size)(rows, resp1, mass1, own)
    edge, resp2, mass2, cost, up2, down2 = call(
        second_kernel,
        (sds((2, size, features), BF16), resp, mass, sds((1, count), F32), one, one),
        (),
        dot * (window + 2) * size,
    )(rows, ids, left, own, right, sums1, mass1, fresh, norm, below1, above1)
    below2, above2 = swap(up2, down2, "own")
    done, part = call(own_kernel, (inner, sds((2, size, features), F32)), (), dot * blocks * size)(
        rows, resp2, mass2, edge, fresh
    )
    out = call(last_kernel, sds((blocks, size, features), BF16))(done, part, mass2, edge, below2, above2)
    cost = cost.reshape(per_pair, pairs).T.reshape(count)
    return out.reshape(centroids.shape), cost


def solution(mesh):
    return jax.shard_map(
        per_device,
        mesh=mesh,
        in_specs=(
            P(("own", "rep"), None),
            P(("own", "rep")),
            P(("own", "rep"), None),
            P("own", "rep", None, None),
        ),
        out_specs=(P("own", "rep", None, None), P(("own", "rep"))),
        check_vma=False,
    )
```

```python
import functools
import math

import jax
import jax.numpy as jnp
from jax import lax
from jax.experimental import pallas as pl
from jax.experimental.pallas import tpu as pltpu
from jax.sharding import PartitionSpec as P

PRIOR = 1.0
LOG2E = 1.4426950408889634
LANES = 128
MASS_ROWS = 16
VMEM = pltpu.VMEM
HBM = pltpu.HBM
ANY = pl.ANY
F32 = jnp.float32
BF16 = jnp.bfloat16


def call(kernel, ins, outs, scratch=(), flops=0, limit=24, aliases=None):
    arrays = [x if space is ANY else pltpu.with_memory_space_constraint(x, space) for x, space in ins]
    made = pl.pallas_call(
        kernel,
        in_specs=[pl.BlockSpec(memory_space=space) for _, space in ins],
        out_shape=[space(*x) if space is not ANY else sds(*x) for x, space in outs],
        out_specs=[pl.BlockSpec(memory_space=space) for _, space in outs],
        scratch_shapes=list(scratch),
        input_output_aliases=aliases or {},
        compiler_params=pltpu.CompilerParams(vmem_limit_bytes=limit << 20),
        cost_estimate=pl.CostEstimate(flops=flops, bytes_accessed=1 << 20, transcendentals=0),
    )(*arrays)
    return made[0] if len(outs) == 1 else made


def sds(shape, dtype):
    return jax.ShapeDtypeStruct(shape, dtype)


def matmul(a, b, contract):
    return lax.dot_general(a, b, (contract, ((), ())), preferred_element_type=F32)


def regroup_kernel(pairs, dest_hbm, rows_hbm, out_hbm, dest_ref, rows_ref, wide, out_ref, in_sems, out_sems):
    count, features = rows_ref.shape
    per_pair = count // pairs
    chunks = features // LANES
    fetch_dest = pltpu.make_async_copy(dest_hbm, dest_ref, in_sems.at[0])
    fetch_rows = pltpu.make_async_copy(rows_hbm, rows_ref, in_sems.at[1])
    fetch_dest.start()
    fetch_rows.start()
    fetch_dest.wait()
    dest = dest_ref[...]
    place = lax.rem(dest, per_pair) * pairs + lax.div(dest, count)
    parts = 4
    step = pairs // parts
    span = step * per_pair * chunks
    rows = None
    stores = []
    for part in range(parts):
        first = part * step
        picks = []
        for slot in range(per_pair):
            ids = lax.broadcasted_iota(jnp.int32, (step, count), 0) + (slot * pairs + first)
            picks.append(jnp.where(ids == place, 1.0, 0.0).astype(BF16))
        pick = jnp.concatenate(picks, axis=0)
        if rows is None:
            fetch_rows.wait()
            rows = rows_ref[...]
        moved = matmul(pick, rows, ((1,), (0,)))
        for slot in range(per_pair):
            for f in range(chunks):
                line = (first * chunks + f) * per_pair + slot
                wide[pl.ds(line, step, stride=chunks * per_pair), :] = moved[
                    slot * step : (slot + 1) * step, f * LANES : (f + 1) * LANES
                ]
        here = pl.ds(part * span, span)
        out_ref[here, :] = wide[here, :].astype(BF16)
        store = pltpu.make_async_copy(out_ref.at[here], out_hbm.at[here], out_sems.at[part])
        store.start()
        stores.append(store)
    for store in stores:
        store.wait()


def unpack_rows(lines_ref, rows_ref, wide, pairs):
    count, features = rows_ref.shape
    per_pair = count // pairs
    chunks = features // LANES
    parts = 4
    step = pairs // parts
    span = step * per_pair * chunks
    for part in range(parts):
        here = pl.ds(part * span, span)
        wide[here, :] = lines_ref[here, :].astype(F32)
        for slot in range(per_pair):
            for f in range(chunks):
                got = wide[pl.ds(part * span + f * per_pair + slot, step, stride=chunks * per_pair), :]
                rows_ref[pl.ds(slot * pairs + part * step, step), f * LANES : (f + 1) * LANES] = got.astype(BF16)


def assign(rows_ref, ids_ref, blocks, norms, resp_ref, tops_ref=None):
    count, features = rows_ref.shape
    window = len(blocks)
    half = 0.5 * LOG2E / math.sqrt(features)
    bias = [norm * half for norm in norms]
    flat = jnp.concatenate(blocks, axis=0)
    per_block = blocks[0].shape[0]
    mass = [0.0] * window
    step = 256
    for start in range(0, count, step):
        rows = rows_ref[pl.ds(start, step), :]
        ids = ids_ref[:, start : start + step]
        cross = matmul(flat, rows, ((1,), (1,)))
        scores = []
        top = None
        for w in range(window):
            hit = jnp.max(jnp.where(ids == w, 0.0, -jnp.inf), axis=0, keepdims=True)
            score = cross[w * per_block : (w + 1) * per_block] * (2.0 * half) - bias[w] + hit
            scores.append(score)
            here = jnp.max(score, axis=0, keepdims=True)
            top = here if top is None else jnp.maximum(top, here)
        total = None
        for w in range(window):
            scores[w] = jnp.exp2(scores[w] - top)
            here = jnp.sum(scores[w], axis=0, keepdims=True)
            total = here if total is None else total + here
        scale = 1.0 / total
        for w in range(window):
            resp = scores[w] * scale
            resp_ref[w * per_block : (w + 1) * per_block, start : start + step] = resp.astype(BF16)
            mass[w] = mass[w] + resp
        if tops_ref is not None:
            tops_ref[:, start : start + step] = top * (1.0 / LOG2E) + jnp.log(total)
    return [jnp.sum(m, axis=1, keepdims=True) for m in mass]


def square_norms(blocks):
    wide = [block.astype(F32) for block in blocks]
    return [jnp.sum(w * w, axis=1, keepdims=True) for w in wide]


def diagonal(size):
    across = lax.broadcasted_iota(jnp.int32, (size, size), 0)
    return across == lax.broadcasted_iota(jnp.int32, (size, size), 1)


def pack_mass(masses):
    size = masses[0].shape[0]
    eye = diagonal(size)
    lines = [jnp.sum(jnp.where(eye, m, 0.0), axis=0, keepdims=True) for m in masses]
    line = jnp.concatenate(lines, axis=1)
    high = line.astype(BF16).astype(F32)
    row = lax.broadcasted_iota(jnp.int32, (MASS_ROWS, line.shape[1]), 0)
    return jnp.where(row == 0, high, jnp.where(row == 1, line - high, 0.0)).astype(BF16)


def unpack_mass(packed, which, size):
    line = packed[:, which * size : (which + 1) * size].astype(F32)
    line = jnp.sum(line, axis=0, keepdims=True)
    return jnp.sum(jnp.where(diagonal(size), line, 0.0), axis=1, keepdims=True)


def package(pkg_ref, sums, masses):
    size = masses[0].shape[0]
    blocks = len(sums)
    for k in range(blocks):
        pkg_ref[k * size : (k + 1) * size, :] = sums[k].astype(BF16)
    packed = pack_mass(masses)
    pkg_ref[blocks * size :, : blocks * size] = packed
    rest = pkg_ref.shape[1] - blocks * size
    pkg_ref[blocks * size :, blocks * size :] = jnp.zeros((MASS_ROWS, rest), BF16)


def refresh(total, tally, previous):
    return ((total + PRIOR * previous.astype(F32)) / (tally + PRIOR)).astype(BF16)


def first_kernel(
    pairs, lines_ref, ids_ref, left_ref, own_ref, right_ref,
    rows_ref, resp_ref, sums_ref, mass_ref, up_ref, down_ref, wide,
):
    blocks = [left_ref[...]] + [own_ref[k] for k in range(own_ref.shape[0])] + [right_ref[...]]
    norms = square_norms(blocks)
    unpack_rows(lines_ref, rows_ref, wide, pairs)
    mass = assign(rows_ref, ids_ref, blocks, norms, resp_ref)
    size = own_ref.shape[1]
    last = len(blocks) - 1
    rows = rows_ref[...]
    sums = []
    for k, w in enumerate((0, 1, last - 1, last)):
        total = matmul(resp_ref[w * size : (w + 1) * size, :], rows, ((1,), (0,)))
        sums_ref[k] = total + PRIOR * blocks[w].astype(F32)
        sums.append(total)
    for w in range(last + 1):
        mass_ref[w * size : (w + 1) * size, :] = mass[w] + PRIOR
    package(up_ref, sums[2:], mass[last - 1 :])
    package(down_ref, sums[:2], mass[:2])


def ratio(total, tally):
    return (total * (1.0 / tally)).astype(BF16)


def inner_kernel(rows_ref, resp_ref, mass_ref, own_ref, fresh_ref, norm_ref):
    blocks, size, _ = own_ref.shape
    rows = rows_ref[...]
    for k in range(1, blocks - 1):
        w = k + 1
        total = matmul(resp_ref[w * size : (w + 1) * size, :], rows, ((1,), (0,)))
        total = total + PRIOR * own_ref[k].astype(F32)
        fresh_ref[k - 1] = ratio(total, mass_ref[w * size : (w + 1) * size, :])
    eye = diagonal(LANES)
    for start in range(0, rows_ref.shape[0], LANES):
        wide = rows_ref[pl.ds(start, LANES), :].astype(F32)
        norm = jnp.sum(wide * wide, axis=1, keepdims=True)
        norm_ref[:, start : start + LANES] = jnp.sum(jnp.where(eye, norm, 0.0), axis=0, keepdims=True)


def second_kernel(
    rows_ref, ids_ref, sums_ref, mass_ref, fresh_ref, norm_ref, below_ref, above_ref,
    edge_ref, resp_ref, mass_out, cost_ref, up_ref, down_ref,
):
    inner, size, _ = fresh_ref.shape
    last = inner + 3
    new = []
    for p, (pkg, ws) in enumerate(((below_ref, (0, 1)), (above_ref, (last - 1, last)))):
        packed = pkg[2 * size :, : 2 * size]
        for k, w in enumerate(ws):
            total = sums_ref[2 * p + k] + pkg[k * size : (k + 1) * size, :].astype(F32)
            tally = mass_ref[w * size : (w + 1) * size, :] + unpack_mass(packed, k, size)
            new.append(ratio(total, tally))
    edge_ref[0] = new[1]
    edge_ref[1] = new[2]
    blocks = new[:2] + [fresh_ref[k] for k in range(inner)] + new[2:]
    mass = assign(rows_ref, ids_ref, blocks, square_norms(blocks), resp_ref, cost_ref)
    half = 0.5 / math.sqrt(rows_ref.shape[1])
    cost_ref[...] = norm_ref[...] * half - cost_ref[...]
    for w in range(last + 1):
        mass_out[w * size : (w + 1) * size, :] = mass[w] + PRIOR
    rows = rows_ref[...]
    for pkg, w in ((up_ref, last), (down_ref, 0)):
        total = matmul(resp_ref[w * size : (w + 1) * size, :], rows, ((1,), (0,)))
        package(pkg, [total], [mass[w]])


def interleave(lines_ref, out_ref, slots):
    count = lines_ref.shape[1]
    pairs = count // slots
    width = LANES * slots
    groups = pairs // LANES
    row = lax.broadcasted_iota(jnp.int32, (width, width), 0)
    lane = lax.broadcasted_iota(jnp.int32, (width, width), 1)
    pick = jnp.where(row == lax.rem(lane, slots) * LANES + lax.div(lane, slots), 1.0, 0.0).astype(BF16)
    pieces = []
    for g in range(groups):
        cuts = [lines_ref[:, s * pairs + g * LANES : s * pairs + (g + 1) * LANES] for s in range(slots)]
        left = jnp.concatenate(cuts, axis=1)
        for _ in range(3):
            piece = left.astype(BF16).astype(F32)
            pieces.append(piece)
            left = left - piece
    pieces += [jnp.zeros_like(pieces[0])] * (-len(pieces) % 16)
    moved = matmul(jnp.concatenate(pieces, axis=0).astype(BF16), pick, ((1,), (0,)))
    for g in range(groups):
        line = moved[3 * g : 3 * g + 1] + moved[3 * g + 1 : 3 * g + 2] + moved[3 * g + 2 : 3 * g + 3]
        for s in range(slots):
            out_ref[g * slots + s : g * slots + s + 1, :] = line[:, s * LANES : (s + 1) * LANES]


def own_kernel(
    slots, rows_ref, resp_ref, mass_ref, edge_ref, fresh_ref, cost_ref, out_hbm, part_ref, placed_ref, done_ref, sem
):
    inner, size, _ = fresh_ref.shape
    rows = rows_ref[...]
    for k in range(inner):
        w = k + 2
        total = matmul(resp_ref[w * size : (w + 1) * size, :], rows, ((1,), (0,)))
        total = total + PRIOR * fresh_ref[k].astype(F32)
        done_ref[k] = ratio(total, mass_ref[w * size : (w + 1) * size, :])
    store = pltpu.make_async_copy(done_ref, out_hbm.at[pl.ds(1, inner)], sem)
    store.start()
    for e, w in ((0, 1), (1, inner + 2)):
        total = matmul(resp_ref[w * size : (w + 1) * size, :], rows, ((1,), (0,)))
        part_ref[e] = total + PRIOR * edge_ref[e].astype(F32)
    interleave(cost_ref, placed_ref, slots)
    store.wait()


def last_kernel(given_hbm, part_ref, mass_ref, below_ref, above_ref, out_hbm, done_ref, sems):
    blocks, size, _ = out_hbm.shape
    stores = []
    for e, (k, pkg) in enumerate(((0, below_ref), (blocks - 1, above_ref))):
        w = k + 1
        total = part_ref[e] + pkg[:size, :].astype(F32)
        tally = mass_ref[w * size : (w + 1) * size, :] + unpack_mass(pkg[size:, :size], 0, size)
        done_ref[e] = ratio(total, tally)
        stores.append(pltpu.make_async_copy(done_ref.at[e], out_hbm.at[k], sems.at[e]))
        stores[-1].start()
    for store in stores:
        store.wait()


def swap(up, down, axis):
    devices = lax.axis_size(axis)
    pairs = [(i, i + 1) for i in range(devices - 1)]
    below = lax.ppermute(up, axis, pairs)
    above = lax.ppermute(down, axis, [(j, i) for i, j in pairs])
    return below, above


def per_device(sample_rows, destination, neighbours, centroids):
    own_count, rep_count = lax.axis_size("own"), lax.axis_size("rep")
    pairs = own_count * rep_count
    count, features = sample_rows.shape
    per_pair = count // pairs
    chunks = features // LANES
    lines = count * chunks
    blocks, _, size, _ = centroids.shape
    window = blocks + 2
    own = centroids.reshape(blocks, size, features)
    wide = pltpu.VMEM((lines + chunks * per_pair + 4, LANES), F32)
    dma = pltpu.SemaphoreType.DMA
    dot = 2 * count * features
    block = (size, features)

    outgoing = call(
        functools.partial(regroup_kernel, pairs),
        [(destination.reshape(1, count), HBM), (sample_rows, HBM)],
        [(((lines, LANES), BF16), HBM)],
        [VMEM((1, count), jnp.int32), VMEM((count, features), BF16), wide, VMEM((lines, LANES), BF16), dma((2,)), dma((4,))],
        dot * count,
    )
    left, right = swap(own[blocks - 1], own[0], "own")
    first_block = lax.axis_index("own") * blocks - 1
    ids = (neighbours // rep_count - first_block).T
    ids = ids.reshape(-1, pairs, per_pair).swapaxes(1, 2).reshape(-1, count)
    arrived = lax.all_to_all(
        outgoing.reshape(pairs, lines // pairs // 4, 4, LANES), ("own", "rep"), split_axis=0, concat_axis=0, tiled=True
    ).reshape(lines, LANES)

    resp = (((window * size, count), BF16), VMEM)
    mass = (((window * size, 1), F32), VMEM)
    two = (((2 * size + MASS_ROWS, features), BF16), VMEM)
    one = (((size + MASS_ROWS, features), BF16), VMEM)
    line = (((1, count), F32), VMEM)
    rows, resp1, sums1, mass1, up1, down1 = call(
        functools.partial(first_kernel, pairs),
        [(arrived, VMEM), (ids, VMEM), (left, VMEM), (own, VMEM), (right, VMEM)],
        [(((count, features), BF16), VMEM), resp, (((4,) + block, F32), VMEM), mass, two, two],
        [wide],
        dot * (window + 4) * size,
    )
    below1, above1 = swap(up1, down1, "own")
    fresh, norm = call(
        inner_kernel,
        [(rows, VMEM), (resp1, VMEM), (mass1, VMEM), (own, VMEM)],
        [(((blocks - 2,) + block, BF16), VMEM), line],
        flops=dot * 2 * size,
    )
    edge, resp2, mass2, cost, up2, down2 = call(
        second_kernel,
        [(x, VMEM) for x in (rows, ids, sums1, mass1, fresh, norm, below1, above1)],
        [(((2,) + block, BF16), VMEM), resp, mass, line, one, one],
        flops=dot * (window + 2) * size,
    )
    below2, above2 = swap(up2, down2, "own")
    given, part, placed = call(
        functools.partial(own_kernel, per_pair),
        [(x, VMEM) for x in (rows, resp2, mass2, edge, fresh, cost)],
        [(((blocks,) + block, BF16), HBM), (((2,) + block, F32), VMEM), (((count // LANES, LANES), F32), VMEM)],
        [VMEM((blocks - 2,) + block, BF16), dma],
        dot * blocks * size,
    )
    out = call(
        last_kernel,
        [(given, HBM), (part, VMEM), (mass2, VMEM), (below2, VMEM), (above2, VMEM)],
        [(((blocks,) + block, BF16), HBM)],
        [VMEM((2,) + block, BF16), dma((2,))],
        aliases={0: 0},
    )
    return out.reshape(centroids.shape), placed.reshape(count)


def solution(mesh):
    return jax.shard_map(
        per_device,
        mesh=mesh,
        in_specs=(
            P(("own", "rep"), None),
            P(("own", "rep")),
            P(("own", "rep"), None),
            P("own", "rep", None, None),
        ),
        out_specs=(P("own", "rep", None, None), P(("own", "rep"))),
        check_vma=False,
    )
```

```python
import functools
import math

import jax
import jax.numpy as jnp
from jax import lax
from jax.experimental import pallas as pl
from jax.experimental.pallas import tpu as pltpu
from jax.sharding import PartitionSpec as P

PRIOR = 1.0
LOG2E = 1.4426950408889634
LANES = 128
MASS_ROWS = 16
VMEM = pltpu.VMEM
HBM = pltpu.HBM
ANY = pl.ANY
F32 = jnp.float32
BF16 = jnp.bfloat16


def call(kernel, ins, outs, scratch=(), flops=0, limit=24, aliases=None):
    arrays = [x if space is ANY else pltpu.with_memory_space_constraint(x, space) for x, space in ins]
    made = pl.pallas_call(
        kernel,
        in_specs=[pl.BlockSpec(memory_space=space) for _, space in ins],
        out_shape=[space(*x) if space is not ANY else sds(*x) for x, space in outs],
        out_specs=[pl.BlockSpec(memory_space=space) for _, space in outs],
        scratch_shapes=list(scratch),
        input_output_aliases=aliases or {},
        compiler_params=pltpu.CompilerParams(vmem_limit_bytes=limit << 20),
        cost_estimate=pl.CostEstimate(flops=flops, bytes_accessed=1 << 20, transcendentals=0),
    )(*arrays)
    return made[0] if len(outs) == 1 else made


def sds(shape, dtype):
    return jax.ShapeDtypeStruct(shape, dtype)


def matmul(a, b, contract):
    return lax.dot_general(a, b, (contract, ((), ())), preferred_element_type=F32)


def regroup_kernel(pairs, dest_hbm, rows_hbm, out_hbm, dest_ref, rows_ref, wide, out_ref, in_sems, out_sems):
    count, features = rows_ref.shape
    per_pair = count // pairs
    chunks = features // LANES
    fetch_dest = pltpu.make_async_copy(dest_hbm, dest_ref, in_sems.at[0])
    fetch_rows = pltpu.make_async_copy(rows_hbm, rows_ref, in_sems.at[1])
    fetch_dest.start()
    fetch_rows.start()
    fetch_dest.wait()
    dest = dest_ref[...]
    place = lax.rem(dest, per_pair) * pairs + lax.div(dest, count)
    parts = 4
    step = pairs // parts
    span = step * per_pair * chunks
    rows = None
    stores = []
    for part in range(parts):
        first = part * step
        picks = []
        for slot in range(per_pair):
            ids = lax.broadcasted_iota(jnp.int32, (step, count), 0) + (slot * pairs + first)
            picks.append(jnp.where(ids == place, 1.0, 0.0).astype(BF16))
        pick = jnp.concatenate(picks, axis=0)
        if rows is None:
            fetch_rows.wait()
            rows = rows_ref[...]
        moved = matmul(pick, rows, ((1,), (0,)))
        for slot in range(per_pair):
            for f in range(chunks):
                line = (first * chunks + f) * per_pair + slot
                wide[pl.ds(line, step, stride=chunks * per_pair), :] = moved[
                    slot * step : (slot + 1) * step, f * LANES : (f + 1) * LANES
                ]
        here = pl.ds(part * span, span)
        out_ref[here, :] = wide[here, :].astype(BF16)
        store = pltpu.make_async_copy(out_ref.at[here], out_hbm.at[here], out_sems.at[part])
        store.start()
        stores.append(store)
    for store in stores:
        store.wait()


def unpack_rows(lines_ref, rows_ref, wide, pairs):
    count, features = rows_ref.shape
    per_pair = count // pairs
    chunks = features // LANES
    parts = 4
    step = pairs // parts
    span = step * per_pair * chunks
    for part in range(parts):
        here = pl.ds(part * span, span)
        wide[here, :] = lines_ref[here, :].astype(F32)
        for slot in range(per_pair):
            for f in range(chunks):
                got = wide[pl.ds(part * span + f * per_pair + slot, step, stride=chunks * per_pair), :]
                rows_ref[pl.ds(slot * pairs + part * step, step), f * LANES : (f + 1) * LANES] = got.astype(BF16)


STEP = 256


def half_scale(features):
    return 0.5 * LOG2E / math.sqrt(features)


def scored(flat, biases, slots, rows, ids):
    cross = matmul(flat, rows, ((1,), (1,)))
    size = flat.shape[0] // len(slots)
    factor = 2.0 * half_scale(flat.shape[1])
    scores = []
    for k, w in enumerate(slots):
        hit = jnp.max(jnp.where(ids == w, 0.0, -jnp.inf), axis=0, keepdims=True)
        scores.append(cross[k * size : (k + 1) * size] * factor + (hit - biases[k]))
    return scores


def highest(scores):
    return functools.reduce(jnp.maximum, [jnp.max(s, axis=0, keepdims=True) for s in scores])


def added(parts):
    return functools.reduce(jnp.add, [jnp.sum(p, axis=0, keepdims=True) for p in parts])


def square_biases(blocks):
    half = half_scale(blocks[0].shape[1])
    wide = [block.astype(F32) for block in blocks]
    return [jnp.sum(w * w, axis=1, keepdims=True) * half for w in wide]


def row_sums(parts):
    return [jnp.sum(p, axis=1, keepdims=True) for p in parts]


def diagonal(size):
    across = lax.broadcasted_iota(jnp.int32, (size, size), 0)
    return across == lax.broadcasted_iota(jnp.int32, (size, size), 1)


def pack_mass(masses):
    size = masses[0].shape[0]
    eye = diagonal(size)
    lines = [jnp.sum(jnp.where(eye, m, 0.0), axis=0, keepdims=True) for m in masses]
    line = jnp.concatenate(lines, axis=1)
    high = line.astype(BF16).astype(F32)
    row = lax.broadcasted_iota(jnp.int32, (MASS_ROWS, line.shape[1]), 0)
    return jnp.where(row == 0, high, jnp.where(row == 1, line - high, 0.0)).astype(BF16)


def unpack_mass(packed, which, size):
    line = packed[:, which * size : (which + 1) * size].astype(F32)
    line = jnp.sum(line, axis=0, keepdims=True)
    return jnp.sum(jnp.where(diagonal(size), line, 0.0), axis=1, keepdims=True)


def package(pkg_ref, sums, masses):
    size = masses[0].shape[0]
    blocks = len(sums)
    for k in range(blocks):
        pkg_ref[k * size : (k + 1) * size, :] = sums[k].astype(BF16)
    packed = pack_mass(masses)
    pkg_ref[blocks * size :, : blocks * size] = packed
    rest = pkg_ref.shape[1] - blocks * size
    pkg_ref[blocks * size :, blocks * size :] = jnp.zeros((MASS_ROWS, rest), BF16)


def refresh(total, tally, previous):
    return ((total + PRIOR * previous.astype(F32)) / (tally + PRIOR)).astype(BF16)


def first_kernel(
    pairs, lines_ref, ids_ref, left_ref, own_ref, right_ref,
    rows_ref, inner_ref, scale_ref, sums_ref, mass_ref, up_ref, down_ref, wide, resp_ref,
):
    blocks = [left_ref[...]] + [own_ref[k] for k in range(own_ref.shape[0])] + [right_ref[...]]
    last = len(blocks) - 1
    size = own_ref.shape[1]
    biases = square_biases(blocks)
    flat = jnp.concatenate(blocks, axis=0)
    unpack_rows(lines_ref, rows_ref, wide, pairs)
    edges = (0, 1, last - 1, last)
    mass = [0.0] * len(edges)
    count = rows_ref.shape[0]
    for start in range(0, count, STEP):
        here = slice(start, start + STEP)
        scores = scored(flat, biases, range(last + 1), rows_ref[here, :], ids_ref[:, here])
        top = highest(scores)
        weights = [jnp.exp2(score - top) for score in scores]
        scale = 1.0 / added(weights)
        scale_ref[:, here] = scale
        for k in range(2, last - 1):
            inner_ref[(k - 2) * size : (k - 1) * size, here] = weights[k]
        for k, w in enumerate(edges):
            resp = weights[w] * scale
            resp_ref[k * size : (k + 1) * size, here] = resp.astype(BF16)
            mass[k] = mass[k] + resp
    mass = row_sums(mass)
    rows = rows_ref[...]
    sums = []
    for k, w in enumerate(edges):
        total = matmul(resp_ref[k * size : (k + 1) * size, :], rows, ((1,), (0,)))
        sums_ref[k] = total + PRIOR * blocks[w].astype(F32)
        sums.append(total)
        mass_ref[k * size : (k + 1) * size, :] = mass[k] + PRIOR
    package(up_ref, sums[2:], mass[2:])
    package(down_ref, sums[:2], mass[:2])


def ratio(total, tally):
    return (total * (1.0 / tally)).astype(BF16)


def inner_kernel(
    rows_ref, ids_ref, inner_ref, scale_ref, own_ref, fresh_ref, norm_ref, next_ref, top_ref, total_ref, resp_ref
):
    blocks, size, _ = own_ref.shape
    inner = blocks - 2
    count = rows_ref.shape[0]
    mass = [0.0] * inner
    for start in range(0, count, STEP):
        here = slice(start, start + STEP)
        for k in range(inner):
            there = slice(k * size, (k + 1) * size)
            resp = inner_ref[there, here] * scale_ref[:, here]
            resp_ref[there, here] = resp.astype(BF16)
            mass[k] = mass[k] + resp
    mass = row_sums(mass)
    rows = rows_ref[...]
    new = []
    for k in range(inner):
        total = matmul(resp_ref[k * size : (k + 1) * size, :], rows, ((1,), (0,)))
        new.append(ratio(total + PRIOR * own_ref[k + 1].astype(F32), mass[k] + PRIOR))
        fresh_ref[k] = new[k]
    biases = square_biases(new)
    flat = jnp.concatenate(new, axis=0)
    for start in range(0, count, STEP):
        here = slice(start, start + STEP)
        scores = scored(flat, biases, range(2, inner + 2), rows_ref[here, :], ids_ref[:, here])
        top = highest(scores)
        top_ref[:, here] = top
        safe = jnp.where(top == -jnp.inf, 0.0, top)
        weights = [jnp.exp2(score - safe) for score in scores]
        total_ref[:, here] = added(weights)
        for k in range(inner):
            next_ref[k * size : (k + 1) * size, here] = weights[k]
    eye = diagonal(LANES)
    for start in range(0, count, LANES):
        wide = rows_ref[start : start + LANES, :].astype(F32)
        norm = jnp.sum(wide * wide, axis=1, keepdims=True)
        norm_ref[:, start : start + LANES] = jnp.sum(jnp.where(eye, norm, 0.0), axis=0, keepdims=True)


def second_kernel(
    rows_ref, ids_ref, sums_ref, mass_ref, norm_ref, top_ref, total_ref, below_ref, above_ref,
    edge_ref, outer_ref, scale_ref, ratio_ref, cost_ref, up_ref, down_ref, resp_ref,
):
    size = sums_ref.shape[1]
    inner = 2
    last = inner + 3
    edges = (0, 1, last - 1, last)
    new = []
    for p, pkg in enumerate((below_ref, above_ref)):
        packed = pkg[2 * size :, : 2 * size]
        for k in range(2):
            e = 2 * p + k
            total = sums_ref[e] + pkg[k * size : (k + 1) * size, :].astype(F32)
            new.append(ratio(total, mass_ref[e * size : (e + 1) * size, :] + unpack_mass(packed, k, size)))
    edge_ref[0] = new[1]
    edge_ref[1] = new[2]
    biases = square_biases(new)
    flat = jnp.concatenate(new, axis=0)
    mass = [0.0, 0.0]
    half = 0.5 / math.sqrt(rows_ref.shape[1])
    for start in range(0, rows_ref.shape[0], STEP):
        here = slice(start, start + STEP)
        scores = scored(flat, biases, edges, rows_ref[here, :], ids_ref[:, here])
        top = jnp.maximum(highest(scores), top_ref[:, here])
        shrink = jnp.exp2(top_ref[:, here] - top)
        weights = [jnp.exp2(score - top) for score in scores]
        total = added(weights) + shrink * total_ref[:, here]
        scale = 1.0 / total
        scale_ref[:, here] = scale
        ratio_ref[:, here] = scale * shrink
        cost_ref[:, here] = norm_ref[:, here] * half - (top * (1.0 / LOG2E) + jnp.log(total))
        for k in range(2):
            outer_ref[k * size : (k + 1) * size, here] = weights[k + 1]
            resp = weights[3 * k] * scale
            resp_ref[k * size : (k + 1) * size, here] = resp.astype(BF16)
            mass[k] = mass[k] + resp
    mass = row_sums(mass)
    rows = rows_ref[...]
    for k, pkg in enumerate((down_ref, up_ref)):
        total = matmul(resp_ref[k * size : (k + 1) * size, :], rows, ((1,), (0,)))
        package(pkg, [total], [mass[k]])


def interleave(lines_ref, out_ref, slots):
    count = lines_ref.shape[1]
    pairs = count // slots
    width = LANES * slots
    groups = pairs // LANES
    row = lax.broadcasted_iota(jnp.int32, (width, width), 0)
    lane = lax.broadcasted_iota(jnp.int32, (width, width), 1)
    pick = jnp.where(row == lax.rem(lane, slots) * LANES + lax.div(lane, slots), 1.0, 0.0).astype(BF16)
    pieces = []
    for g in range(groups):
        cuts = [lines_ref[:, s * pairs + g * LANES : s * pairs + (g + 1) * LANES] for s in range(slots)]
        left = jnp.concatenate(cuts, axis=1)
        for _ in range(3):
            piece = left.astype(BF16).astype(F32)
            pieces.append(piece)
            left = left - piece
    pieces += [jnp.zeros_like(pieces[0])] * (-len(pieces) % 16)
    moved = matmul(jnp.concatenate(pieces, axis=0).astype(BF16), pick, ((1,), (0,)))
    for g in range(groups):
        line = moved[3 * g : 3 * g + 1] + moved[3 * g + 1 : 3 * g + 2] + moved[3 * g + 2 : 3 * g + 3]
        for s in range(slots):
            out_ref[g * slots + s : g * slots + s + 1, :] = line[:, s * LANES : (s + 1) * LANES]


def own_kernel(
    slots, rows_ref, inner_ref, ratio_ref, outer_ref, scale_ref, edge_ref, fresh_ref, cost_ref,
    out_hbm, part_ref, mass_ref, placed_ref, done_ref, resp_ref, sem,
):
    inner, size, _ = fresh_ref.shape
    rows = rows_ref[...]

    def summed(weights_ref, by_ref, blocks):
        mass = [0.0] * blocks
        for start in range(0, rows_ref.shape[0], STEP):
            here = slice(start, start + STEP)
            for k in range(blocks):
                there = slice(k * size, (k + 1) * size)
                resp = weights_ref[there, here] * by_ref[:, here]
                resp_ref[there, here] = resp.astype(BF16)
                mass[k] = mass[k] + resp
        sums = [matmul(resp_ref[k * size : (k + 1) * size, :], rows, ((1,), (0,))) for k in range(blocks)]
        return sums, row_sums(mass)

    sums, mass = summed(inner_ref, ratio_ref, inner)
    for k in range(inner):
        done_ref[k] = ratio(sums[k] + PRIOR * fresh_ref[k].astype(F32), mass[k] + PRIOR)
    store = pltpu.make_async_copy(done_ref, out_hbm.at[pl.ds(1, inner)], sem)
    store.start()
    sums, mass = summed(outer_ref, scale_ref, 2)
    for k in range(2):
        part_ref[k] = sums[k] + PRIOR * edge_ref[k].astype(F32)
        mass_ref[k * size : (k + 1) * size, :] = mass[k] + PRIOR
    interleave(cost_ref, placed_ref, slots)
    store.wait()


def last_kernel(given_hbm, part_ref, mass_ref, below_ref, above_ref, out_hbm, done_ref, sems):
    blocks, size, _ = out_hbm.shape
    stores = []
    for e, (k, pkg) in enumerate(((0, below_ref), (blocks - 1, above_ref))):
        total = part_ref[e] + pkg[:size, :].astype(F32)
        tally = mass_ref[e * size : (e + 1) * size, :] + unpack_mass(pkg[size:, :size], 0, size)
        done_ref[e] = ratio(total, tally)
        stores.append(pltpu.make_async_copy(done_ref.at[e], out_hbm.at[k], sems.at[e]))
        stores[-1].start()
    for store in stores:
        store.wait()


def wide_lines(lines, stride):
    return pltpu.VMEM((lines + stride + 4, LANES), F32)


def run_regroup(pairs, dest, rows):
    count, features = rows.shape
    lines = count * features // LANES
    dma = pltpu.SemaphoreType.DMA
    return call(
        functools.partial(regroup_kernel, pairs),
        [(dest, HBM), (rows, HBM)],
        [(((lines, LANES), BF16), HBM)],
        [
            VMEM((1, count), jnp.int32),
            VMEM((count, features), BF16),
            wide_lines(lines, lines // pairs),
            VMEM((lines, LANES), BF16),
            dma((2,)),
            dma((4,)),
        ],
        2 * count * features * count,
    )


def run_first(pairs, arrived, ids, left, own, right):
    lines, count = arrived.shape[0], ids.shape[1]
    blocks, size, features = own.shape
    window = blocks + 2
    two = (((2 * size + MASS_ROWS, features), BF16), VMEM)
    return call(
        functools.partial(first_kernel, pairs),
        [(arrived, VMEM), (ids, VMEM), (left, VMEM), (own, VMEM), (right, VMEM)],
        [
            (((count, features), BF16), VMEM),
            ((((blocks - 2) * size, count), F32), VMEM),
            (((1, count), F32), VMEM),
            (((4, size, features), F32), VMEM),
            (((4 * size, 1), F32), VMEM),
            two,
            two,
        ],
        [wide_lines(lines, lines // pairs), VMEM((4 * size, count), BF16)],
        2 * count * features * (window + 4) * size,
    )


def run_inner(rows, ids, inner, scale, own):
    blocks, size, features = own.shape
    count = rows.shape[0]
    line = (((1, count), F32), VMEM)
    return call(
        inner_kernel,
        [(x, VMEM) for x in (rows, ids, inner, scale, own)],
        [(((blocks - 2, size, features), BF16), VMEM), line, ((inner.shape, F32), VMEM), line, line],
        [VMEM(inner.shape, BF16)],
        2 * count * features * 4 * size,
    )


def run_second(rows, ids, sums, mass, norm, top, total, below, above):
    _, size, features = sums.shape
    count = rows.shape[0]
    line = (((1, count), F32), VMEM)
    one = (((size + MASS_ROWS, features), BF16), VMEM)
    return call(
        second_kernel,
        [(x, VMEM) for x in (rows, ids, sums, mass, norm, top, total, below, above)],
        [(((2, size, features), BF16), VMEM), (((2 * size, count), F32), VMEM), line, line, line, one, one],
        [VMEM((2 * size, count), BF16)],
        2 * count * features * 6 * size,
    )


def run_own(slots, rows, inner, ratios, outer, scale, edge, fresh, cost):
    blocks, size, features = fresh.shape[0] + 2, fresh.shape[1], fresh.shape[2]
    count = rows.shape[0]
    return call(
        functools.partial(own_kernel, slots),
        [(x, VMEM) for x in (rows, inner, ratios, outer, scale, edge, fresh, cost)],
        [
            (((blocks, size, features), BF16), HBM),
            (((2, size, features), F32), VMEM),
            (((2 * size, 1), F32), VMEM),
            (((count // LANES, LANES), F32), VMEM),
        ],
        [VMEM((blocks - 2, size, features), BF16), VMEM((2 * size, count), BF16), pltpu.SemaphoreType.DMA],
        2 * count * features * blocks * size,
    )


def run_last(given, part, mass, below, above):
    return call(
        last_kernel,
        [(given, HBM)] + [(x, VMEM) for x in (part, mass, below, above)],
        [((given.shape, BF16), HBM)],
        [VMEM(part.shape, BF16), pltpu.SemaphoreType.DMA((2,))],
        aliases={0: 0},
    )


def swap(up, down, axis):
    devices = lax.axis_size(axis)
    pairs = [(i, i + 1) for i in range(devices - 1)]
    below = lax.ppermute(up, axis, pairs)
    above = lax.ppermute(down, axis, [(j, i) for i, j in pairs])
    return below, above


def per_device(sample_rows, destination, neighbours, centroids):
    own_count, rep_count = lax.axis_size("own"), lax.axis_size("rep")
    pairs = own_count * rep_count
    count, features = sample_rows.shape
    per_pair = count // pairs
    chunks = features // LANES
    lines = count * chunks
    blocks, _, size, _ = centroids.shape
    own = centroids.reshape(blocks, size, features)
    outgoing = run_regroup(pairs, destination.reshape(1, count), sample_rows)
    left, right = swap(own[blocks - 1], own[0], "own")
    first_block = lax.axis_index("own") * blocks - 1
    ids = (neighbours // rep_count - first_block).T
    ids = ids.reshape(-1, pairs, per_pair).swapaxes(1, 2).reshape(-1, count)
    arrived = lax.all_to_all(
        outgoing.reshape(pairs, lines // pairs // 4, 4, LANES), ("own", "rep"), split_axis=0, concat_axis=0, tiled=True
    ).reshape(lines, LANES)

    rows, inner1, scale1, sums1, mass1, up1, down1 = run_first(pairs, arrived, ids, left, own, right)
    below1, above1 = swap(up1, down1, "own")
    fresh, norm, inner2, top, total = run_inner(rows, ids, inner1, scale1, own)
    edge, outer, scale2, ratio2, cost, up2, down2 = run_second(rows, ids, sums1, mass1, norm, top, total, below1, above1)
    below2, above2 = swap(up2, down2, "own")
    given, part, mass2, placed = run_own(per_pair, rows, inner2, ratio2, outer, scale2, edge, fresh, cost)
    out = run_last(given, part, mass2, below2, above2)
    return out.reshape(centroids.shape), placed.reshape(count)


def solution(mesh):
    return jax.shard_map(
        per_device,
        mesh=mesh,
        in_specs=(
            P(("own", "rep"), None),
            P(("own", "rep")),
            P(("own", "rep"), None),
            P("own", "rep", None, None),
        ),
        out_specs=(P("own", "rep", None, None), P(("own", "rep"))),
        check_vma=False,
    )
```

```python
import functools
import math

import jax
import jax.numpy as jnp
from jax import lax
from jax.experimental import pallas as pl
from jax.experimental.pallas import tpu as pltpu
from jax.sharding import PartitionSpec as P

PRIOR = 1.0
LOG2E = 1.4426950408889634
LANES = 128
MASS_ROWS = 16
VMEM = pltpu.VMEM
HBM = pltpu.HBM
ANY = pl.ANY
F32 = jnp.float32
BF16 = jnp.bfloat16


def call(kernel, ins, outs, scratch=(), flops=0, limit=24, aliases=None):
    arrays = [x if space is ANY else pltpu.with_memory_space_constraint(x, space) for x, space in ins]
    made = pl.pallas_call(
        kernel,
        in_specs=[pl.BlockSpec(memory_space=space) for _, space in ins],
        out_shape=[space(*x) if space is not ANY else sds(*x) for x, space in outs],
        out_specs=[pl.BlockSpec(memory_space=space) for _, space in outs],
        scratch_shapes=list(scratch),
        input_output_aliases=aliases or {},
        compiler_params=pltpu.CompilerParams(vmem_limit_bytes=limit << 20),
        cost_estimate=pl.CostEstimate(flops=flops, bytes_accessed=1 << 20, transcendentals=0),
    )(*arrays)
    return made[0] if len(outs) == 1 else made


def sds(shape, dtype):
    return jax.ShapeDtypeStruct(shape, dtype)


def matmul(a, b, contract):
    return lax.dot_general(a, b, (contract, ((), ())), preferred_element_type=F32)


def regroup_kernel(pairs, dest_hbm, rows_hbm, out_hbm, dest_ref, rows_ref, wide, out_ref, in_sems, out_sems):
    count, features = rows_ref.shape
    per_pair = count // pairs
    chunks = features // LANES
    fetch_dest = pltpu.make_async_copy(dest_hbm, dest_ref, in_sems.at[0])
    fetch_rows = pltpu.make_async_copy(rows_hbm, rows_ref, in_sems.at[1])
    fetch_dest.start()
    fetch_rows.start()
    fetch_dest.wait()
    dest = dest_ref[...]
    place = lax.rem(dest, per_pair) * pairs + lax.div(dest, count)
    parts = 4
    step = pairs // parts
    span = step * per_pair * chunks
    rows = None
    stores = []
    for part in range(parts):
        first = part * step
        picks = []
        for slot in range(per_pair):
            ids = lax.broadcasted_iota(jnp.int32, (step, count), 0) + (slot * pairs + first)
            picks.append(jnp.where(ids == place, 1.0, 0.0).astype(BF16))
        pick = jnp.concatenate(picks, axis=0)
        if rows is None:
            fetch_rows.wait()
            rows = rows_ref[...]
        moved = matmul(pick, rows, ((1,), (0,)))
        for slot in range(per_pair):
            for f in range(chunks):
                line = (first * chunks + f) * per_pair + slot
                wide[pl.ds(line, step, stride=chunks * per_pair), :] = moved[
                    slot * step : (slot + 1) * step, f * LANES : (f + 1) * LANES
                ]
        here = pl.ds(part * span, span)
        out_ref[here, :] = wide[here, :].astype(BF16)
        store = pltpu.make_async_copy(out_ref.at[here], out_hbm.at[here], out_sems.at[part])
        store.start()
        stores.append(store)
    for store in stores:
        store.wait()


def unpack_rows(lines_ref, rows_ref, wide, pairs):
    count, features = rows_ref.shape
    per_pair = count // pairs
    chunks = features // LANES
    parts = 4
    step = pairs // parts
    span = step * per_pair * chunks
    for part in range(parts):
        here = pl.ds(part * span, span)
        wide[here, :] = lines_ref[here, :].astype(F32)
        for slot in range(per_pair):
            for f in range(chunks):
                got = wide[pl.ds(part * span + f * per_pair + slot, step, stride=chunks * per_pair), :]
                rows_ref[pl.ds(slot * pairs + part * step, step), f * LANES : (f + 1) * LANES] = got.astype(BF16)


STEP = 256


def half_scale(features):
    return 0.5 * LOG2E / math.sqrt(features)


def scored(flat, biases, slots, rows, ids):
    cross = matmul(flat, rows, ((1,), (1,)))
    size = flat.shape[0] // len(slots)
    factor = 2.0 * half_scale(flat.shape[1])
    scores = []
    for k, w in enumerate(slots):
        hit = jnp.max(jnp.where(ids == w, 0.0, -jnp.inf), axis=0, keepdims=True)
        scores.append(cross[k * size : (k + 1) * size] * factor + (hit - biases[k]))
    return scores


def highest(scores):
    return functools.reduce(jnp.maximum, [jnp.max(s, axis=0, keepdims=True) for s in scores])


def added(parts):
    return functools.reduce(jnp.add, [jnp.sum(p, axis=0, keepdims=True) for p in parts])


def square_biases(blocks):
    half = half_scale(blocks[0].shape[1])
    wide = [block.astype(F32) for block in blocks]
    return [jnp.sum(w * w, axis=1, keepdims=True) * half for w in wide]


def row_sums(parts):
    return [jnp.sum(p, axis=1, keepdims=True) for p in parts]


def diagonal(size):
    across = lax.broadcasted_iota(jnp.int32, (size, size), 0)
    return across == lax.broadcasted_iota(jnp.int32, (size, size), 1)


def pack_mass(masses):
    size = masses[0].shape[0]
    eye = diagonal(size)
    lines = [jnp.sum(jnp.where(eye, m, 0.0), axis=0, keepdims=True) for m in masses]
    line = jnp.concatenate(lines, axis=1)
    high = line.astype(BF16).astype(F32)
    row = lax.broadcasted_iota(jnp.int32, (MASS_ROWS, line.shape[1]), 0)
    return jnp.where(row == 0, high, jnp.where(row == 1, line - high, 0.0)).astype(BF16)


def unpack_mass(packed, which, size):
    line = packed[:, which * size : (which + 1) * size].astype(F32)
    line = jnp.sum(line, axis=0, keepdims=True)
    return jnp.sum(jnp.where(diagonal(size), line, 0.0), axis=1, keepdims=True)


def package(pkg_ref, sums, masses):
    size = masses[0].shape[0]
    blocks = len(sums)
    for k in range(blocks):
        pkg_ref[k * size : (k + 1) * size, :] = sums[k].astype(BF16)
    packed = pack_mass(masses)
    pkg_ref[blocks * size :, : blocks * size] = packed
    rest = pkg_ref.shape[1] - blocks * size
    pkg_ref[blocks * size :, blocks * size :] = jnp.zeros((MASS_ROWS, rest), BF16)


def refresh(total, tally, previous):
    return ((total + PRIOR * previous.astype(F32)) / (tally + PRIOR)).astype(BF16)


def arrival_kernel(
    pairs, lines_ref, ids_ref, own_ref, rows_ref, weights_ref, top_ref, total_ref, wide
):
    blocks, size, _ = own_ref.shape
    own = [own_ref[k] for k in range(blocks)]
    biases = square_biases(own)
    flat = jnp.concatenate(own, axis=0)
    unpack_rows(lines_ref, rows_ref, wide, pairs)
    for start in range(0, rows_ref.shape[0], STEP):
        here = slice(start, start + STEP)
        scores = scored(flat, biases, range(1, blocks + 1), rows_ref[here, :], ids_ref[:, here])
        top = highest(scores)
        top_ref[:, here] = top
        weights = [jnp.exp2(score - top) for score in scores]
        total_ref[:, here] = added(weights)
        for k in range(blocks):
            weights_ref[k * size : (k + 1) * size, here] = weights[k]


def first_kernel(
    rows_ref, ids_ref, weights_ref, top_ref, total_ref, left_ref, own_ref, right_ref,
    scale_ref, sums_ref, mass_ref, up_ref, down_ref, resp_ref,
):
    count_own, size, _ = own_ref.shape
    last = count_own + 1
    halo = [left_ref[...], right_ref[...]]
    biases = square_biases(halo)
    flat = jnp.concatenate(halo, axis=0)
    edges = (halo[0], own_ref[0], own_ref[count_own - 1], halo[1])
    mass = [0.0] * len(edges)
    for start in range(0, rows_ref.shape[0], STEP):
        here = slice(start, start + STEP)
        scores = scored(flat, biases, (0, last), rows_ref[here, :], ids_ref[:, here])
        top = jnp.maximum(highest(scores), top_ref[:, here])
        shrink = jnp.exp2(top_ref[:, here] - top)
        weights = [jnp.exp2(score - top) for score in scores]
        scale = 1.0 / (added(weights) + shrink * total_ref[:, here])
        own_scale = shrink * scale
        scale_ref[:, here] = own_scale
        resps = (
            weights[0] * scale,
            weights_ref[:size, here] * own_scale,
            weights_ref[(count_own - 1) * size :, here] * own_scale,
            weights[1] * scale,
        )
        for k, resp in enumerate(resps):
            resp_ref[k * size : (k + 1) * size, here] = resp.astype(BF16)
            mass[k] = mass[k] + resp
    mass = row_sums(mass)
    rows = rows_ref[...]
    sums = []
    for k, block in enumerate(edges):
        total = matmul(resp_ref[k * size : (k + 1) * size, :], rows, ((1,), (0,)))
        sums_ref[k] = total + PRIOR * block.astype(F32)
        sums.append(total)
        mass_ref[k * size : (k + 1) * size, :] = mass[k] + PRIOR
    package(up_ref, sums[2:], mass[2:])
    package(down_ref, sums[:2], mass[:2])


def ratio(total, tally):
    return (total * (1.0 / tally)).astype(BF16)


def inner_kernel(
    rows_ref, ids_ref, weights_ref, scale_ref, own_ref, fresh_ref, norm_ref, next_ref, top_ref, total_ref, resp_ref
):
    blocks, size, _ = own_ref.shape
    inner = blocks - 2
    count = rows_ref.shape[0]
    mass = [0.0] * inner
    for start in range(0, count, STEP):
        here = slice(start, start + STEP)
        for k in range(inner):
            there = slice(k * size, (k + 1) * size)
            resp = weights_ref[(k + 1) * size : (k + 2) * size, here] * scale_ref[:, here]
            resp_ref[there, here] = resp.astype(BF16)
            mass[k] = mass[k] + resp
    mass = row_sums(mass)
    rows = rows_ref[...]
    new = []
    for k in range(inner):
        total = matmul(resp_ref[k * size : (k + 1) * size, :], rows, ((1,), (0,)))
        new.append(ratio(total + PRIOR * own_ref[k + 1].astype(F32), mass[k] + PRIOR))
        fresh_ref[k] = new[k]
    biases = square_biases(new)
    flat = jnp.concatenate(new, axis=0)
    for start in range(0, count, STEP):
        here = slice(start, start + STEP)
        scores = scored(flat, biases, range(2, inner + 2), rows_ref[here, :], ids_ref[:, here])
        top = highest(scores)
        top_ref[:, here] = top
        safe = jnp.where(top == -jnp.inf, 0.0, top)
        weights = [jnp.exp2(score - safe) for score in scores]
        total_ref[:, here] = added(weights)
        for k in range(inner):
            next_ref[k * size : (k + 1) * size, here] = weights[k]
    eye = diagonal(LANES)
    for start in range(0, count, LANES):
        wide = rows_ref[start : start + LANES, :].astype(F32)
        norm = jnp.sum(wide * wide, axis=1, keepdims=True)
        norm_ref[:, start : start + LANES] = jnp.sum(jnp.where(eye, norm, 0.0), axis=0, keepdims=True)


def renewed(pkg_ref, sums, masses):
    size = sums[0].shape[0]
    packed = pkg_ref[2 * size :, : 2 * size]
    new = []
    for k in range(2):
        total = sums[k] + pkg_ref[k * size : (k + 1) * size, :].astype(F32)
        new.append(ratio(total, masses[k] + unpack_mass(packed, k, size)))
    return new


def below_kernel(
    rows_ref, ids_ref, sums_ref, mass_ref, top_ref, total_ref, below_ref,
    edge_ref, weights_ref, new_top_ref, new_total_ref, shrink_ref,
):
    size = sums_ref.shape[1]
    new = renewed(below_ref, [sums_ref[k] for k in range(2)], [mass_ref[k * size : (k + 1) * size, :] for k in range(2)])
    edge_ref[...] = new[1]
    biases = square_biases(new)
    flat = jnp.concatenate(new, axis=0)
    for start in range(0, rows_ref.shape[0], STEP):
        here = slice(start, start + STEP)
        scores = scored(flat, biases, (0, 1), rows_ref[here, :], ids_ref[:, here])
        before = top_ref[:, here]
        top = jnp.maximum(highest(scores), before)
        safe = jnp.where(top == -jnp.inf, 0.0, top)
        shrink = jnp.exp2(before - safe)
        weights = [jnp.exp2(score - safe) for score in scores]
        new_top_ref[:, here] = top
        shrink_ref[:, here] = shrink
        new_total_ref[:, here] = added(weights) + shrink * total_ref[:, here]
        for k in range(2):
            weights_ref[k * size : (k + 1) * size, here] = weights[k]


def above_kernel(
    rows_ref, ids_ref, sums_ref, mass_ref, norm_ref, top_ref, total_ref, shrink_ref, weights_ref, above_ref,
    edge_ref, outer_ref, above_scale_ref, below_scale_ref, inner_scale_ref, cost_ref, up_ref, down_ref, resp_ref,
):
    size = sums_ref.shape[1]
    last = 5
    new = renewed(
        above_ref, [sums_ref[k] for k in range(2, 4)], [mass_ref[k * size : (k + 1) * size, :] for k in range(2, 4)]
    )
    edge_ref[...] = new[0]
    biases = square_biases(new)
    flat = jnp.concatenate(new, axis=0)
    mass = [0.0, 0.0]
    half = 0.5 / math.sqrt(rows_ref.shape[1])
    for start in range(0, rows_ref.shape[0], STEP):
        here = slice(start, start + STEP)
        scores = scored(flat, biases, (last - 1, last), rows_ref[here, :], ids_ref[:, here])
        before = top_ref[:, here]
        top = jnp.maximum(highest(scores), before)
        fade = jnp.exp2(before - top)
        weights = [jnp.exp2(score - top) for score in scores]
        total = added(weights) + fade * total_ref[:, here]
        scale = 1.0 / total
        below_scale = scale * fade
        above_scale_ref[:, here] = scale
        below_scale_ref[:, here] = below_scale
        inner_scale_ref[:, here] = below_scale * shrink_ref[:, here]
        cost_ref[:, here] = norm_ref[:, here] * half - (top * (1.0 / LOG2E) + jnp.log(total))
        outer_ref[:, here] = weights[0]
        for k, resp in enumerate((weights_ref[:size, here] * below_scale, weights[1] * scale)):
            resp_ref[k * size : (k + 1) * size, here] = resp.astype(BF16)
            mass[k] = mass[k] + resp
    mass = row_sums(mass)
    rows = rows_ref[...]
    for k, pkg in enumerate((down_ref, up_ref)):
        total = matmul(resp_ref[k * size : (k + 1) * size, :], rows, ((1,), (0,)))
        package(pkg, [total], [mass[k]])


def interleave(lines_ref, out_ref, slots):
    count = lines_ref.shape[1]
    pairs = count // slots
    width = LANES * slots
    groups = pairs // LANES
    row = lax.broadcasted_iota(jnp.int32, (width, width), 0)
    lane = lax.broadcasted_iota(jnp.int32, (width, width), 1)
    pick = jnp.where(row == lax.rem(lane, slots) * LANES + lax.div(lane, slots), 1.0, 0.0).astype(BF16)
    pieces = []
    for g in range(groups):
        cuts = [lines_ref[:, s * pairs + g * LANES : s * pairs + (g + 1) * LANES] for s in range(slots)]
        left = jnp.concatenate(cuts, axis=1)
        for _ in range(3):
            piece = left.astype(BF16).astype(F32)
            pieces.append(piece)
            left = left - piece
    pieces += [jnp.zeros_like(pieces[0])] * (-len(pieces) % 16)
    moved = matmul(jnp.concatenate(pieces, axis=0).astype(BF16), pick, ((1,), (0,)))
    for g in range(groups):
        line = moved[3 * g : 3 * g + 1] + moved[3 * g + 1 : 3 * g + 2] + moved[3 * g + 2 : 3 * g + 3]
        for s in range(slots):
            out_ref[g * slots + s : g * slots + s + 1, :] = line[:, s * LANES : (s + 1) * LANES]


def own_kernel(
    slots, rows_ref, inner_ref, inner_scale_ref, below_ref, below_scale_ref, above_ref, above_scale_ref,
    below_edge_ref, above_edge_ref, fresh_ref, cost_ref,
    out_hbm, part_ref, mass_ref, placed_ref, done_ref, resp_ref, sem,
):
    inner, size, _ = fresh_ref.shape
    rows = rows_ref[...]

    def summed(weights):
        mass = [0.0] * len(weights)
        for start in range(0, rows_ref.shape[0], STEP):
            here = slice(start, start + STEP)
            for k, (ref, first, by_ref) in enumerate(weights):
                resp = ref[first : first + size, here] * by_ref[:, here]
                resp_ref[k * size : (k + 1) * size, here] = resp.astype(BF16)
                mass[k] = mass[k] + resp
        sums = [
            matmul(resp_ref[k * size : (k + 1) * size, :], rows, ((1,), (0,))) for k in range(len(weights))
        ]
        return sums, row_sums(mass)

    sums, mass = summed([(inner_ref, k * size, inner_scale_ref) for k in range(inner)])
    for k in range(inner):
        done_ref[k] = ratio(sums[k] + PRIOR * fresh_ref[k].astype(F32), mass[k] + PRIOR)
    store = pltpu.make_async_copy(done_ref, out_hbm.at[pl.ds(1, inner)], sem)
    store.start()
    sums, mass = summed([(below_ref, size, below_scale_ref), (above_ref, 0, above_scale_ref)])
    for k, edge_ref in enumerate((below_edge_ref, above_edge_ref)):
        part_ref[k] = sums[k] + PRIOR * edge_ref[...].astype(F32)
        mass_ref[k * size : (k + 1) * size, :] = mass[k] + PRIOR
    interleave(cost_ref, placed_ref, slots)
    store.wait()


def last_kernel(given_hbm, part_ref, mass_ref, below_ref, above_ref, out_hbm, done_ref, sems):
    blocks, size, _ = out_hbm.shape
    stores = []
    for e, (k, pkg) in enumerate(((0, below_ref), (blocks - 1, above_ref))):
        total = part_ref[e] + pkg[:size, :].astype(F32)
        tally = mass_ref[e * size : (e + 1) * size, :] + unpack_mass(pkg[size:, :size], 0, size)
        done_ref[e] = ratio(total, tally)
        stores.append(pltpu.make_async_copy(done_ref.at[e], out_hbm.at[k], sems.at[e]))
        stores[-1].start()
    for store in stores:
        store.wait()


def wide_lines(lines, stride):
    return pltpu.VMEM((lines + stride + 4, LANES), F32)


def run_regroup(pairs, dest, rows):
    count, features = rows.shape
    lines = count * features // LANES
    dma = pltpu.SemaphoreType.DMA
    return call(
        functools.partial(regroup_kernel, pairs),
        [(dest, HBM), (rows, HBM)],
        [(((lines, LANES), BF16), HBM)],
        [
            VMEM((1, count), jnp.int32),
            VMEM((count, features), BF16),
            wide_lines(lines, lines // pairs),
            VMEM((lines, LANES), BF16),
            dma((2,)),
            dma((4,)),
        ],
        2 * count * features * count,
    )


def run_arrival(pairs, arrived, ids, own):
    lines, count = arrived.shape[0], ids.shape[1]
    blocks, size, features = own.shape
    line = (((1, count), F32), VMEM)
    return call(
        functools.partial(arrival_kernel, pairs),
        [(arrived, VMEM), (ids, VMEM), (own, VMEM)],
        [(((count, features), BF16), VMEM), (((blocks * size, count), F32), VMEM), line, line],
        [wide_lines(lines, lines // pairs)],
        2 * count * features * blocks * size,
    )


def run_first(rows, ids, weights, top, total, left, own, right):
    blocks, size, features = own.shape
    count = rows.shape[0]
    two = (((2 * size + MASS_ROWS, features), BF16), VMEM)
    return call(
        first_kernel,
        [(x, VMEM) for x in (rows, ids, weights, top, total, left, own, right)],
        [(((1, count), F32), VMEM), (((4, size, features), F32), VMEM), (((4 * size, 1), F32), VMEM), two, two],
        [VMEM((4 * size, count), BF16)],
        2 * count * features * 6 * size,
    )


def run_inner(rows, ids, weights, scale, own):
    blocks, size, features = own.shape
    count = rows.shape[0]
    inner = (blocks - 2) * size
    line = (((1, count), F32), VMEM)
    return call(
        inner_kernel,
        [(x, VMEM) for x in (rows, ids, weights, scale, own)],
        [(((blocks - 2, size, features), BF16), VMEM), line, (((inner, count), F32), VMEM), line, line],
        [VMEM((inner, count), BF16)],
        2 * count * features * 4 * size,
    )


def run_below(rows, ids, sums, mass, top, total, below):
    _, size, features = sums.shape
    count = rows.shape[0]
    line = (((1, count), F32), VMEM)
    return call(
        below_kernel,
        [(x, VMEM) for x in (rows, ids, sums, mass, top, total, below)],
        [(((size, features), BF16), VMEM), (((2 * size, count), F32), VMEM), line, line, line],
        flops=2 * count * features * 2 * size,
    )


def run_above(rows, ids, sums, mass, norm, top, total, shrink, weights, above):
    _, size, features = sums.shape
    count = rows.shape[0]
    line = (((1, count), F32), VMEM)
    one = (((size + MASS_ROWS, features), BF16), VMEM)
    return call(
        above_kernel,
        [(x, VMEM) for x in (rows, ids, sums, mass, norm, top, total, shrink, weights, above)],
        [(((size, features), BF16), VMEM), (((size, count), F32), VMEM), line, line, line, line, one, one],
        [VMEM((2 * size, count), BF16)],
        2 * count * features * 4 * size,
    )


def run_own(slots, rows, inner, inner_scale, below, below_scale, above, above_scale, below_edge, above_edge, fresh, cost):
    blocks, size, features = fresh.shape[0] + 2, fresh.shape[1], fresh.shape[2]
    count = rows.shape[0]
    ins = (rows, inner, inner_scale, below, below_scale, above, above_scale, below_edge, above_edge, fresh, cost)
    return call(
        functools.partial(own_kernel, slots),
        [(x, VMEM) for x in ins],
        [
            (((blocks, size, features), BF16), HBM),
            (((2, size, features), F32), VMEM),
            (((2 * size, 1), F32), VMEM),
            (((count // LANES, LANES), F32), VMEM),
        ],
        [VMEM((blocks - 2, size, features), BF16), VMEM((2 * size, count), BF16), pltpu.SemaphoreType.DMA],
        2 * count * features * blocks * size,
    )


def run_last(given, part, mass, below, above):
    return call(
        last_kernel,
        [(given, HBM)] + [(x, VMEM) for x in (part, mass, below, above)],
        [((given.shape, BF16), HBM)],
        [VMEM(part.shape, BF16), pltpu.SemaphoreType.DMA((2,))],
        aliases={0: 0},
    )


def swap(up, down, axis):
    devices = lax.axis_size(axis)
    pairs = [(i, i + 1) for i in range(devices - 1)]
    below = lax.ppermute(up, axis, pairs)
    above = lax.ppermute(down, axis, [(j, i) for i, j in pairs])
    return below, above


def per_device(sample_rows, destination, neighbours, centroids):
    own_count, rep_count = lax.axis_size("own"), lax.axis_size("rep")
    pairs = own_count * rep_count
    count, features = sample_rows.shape
    per_pair = count // pairs
    chunks = features // LANES
    lines = count * chunks
    blocks, _, size, _ = centroids.shape
    own = centroids.reshape(blocks, size, features)
    outgoing = run_regroup(pairs, destination.reshape(1, count), sample_rows)
    left, right = swap(own[blocks - 1], own[0], "own")
    first_block = lax.axis_index("own") * blocks - 1
    ids = (neighbours // rep_count - first_block).T
    ids = ids.reshape(-1, pairs, per_pair).swapaxes(1, 2).reshape(-1, count)
    arrived = lax.all_to_all(
        outgoing.reshape(pairs, lines // pairs // 4, 4, LANES), ("own", "rep"), split_axis=0, concat_axis=0, tiled=True
    ).reshape(lines, LANES)

    rows, weights1, top1, total1 = run_arrival(pairs, arrived, ids, own)
    scale1, sums1, mass1, up1, down1 = run_first(rows, ids, weights1, top1, total1, left, own, right)
    below1, above1 = swap(up1, down1, "own")
    fresh, norm, inner2, top, total = run_inner(rows, ids, weights1, scale1, own)
    below_edge, below_w, top, total, shrink = run_below(rows, ids, sums1, mass1, top, total, below1)
    above_edge, above_w, above_by, below_by, inner_by, cost, up2, down2 = run_above(
        rows, ids, sums1, mass1, norm, top, total, shrink, below_w, above1
    )
    below2, above2 = swap(up2, down2, "own")
    given, part, mass2, placed = run_own(
        per_pair, rows, inner2, inner_by, below_w, below_by, above_w, above_by, below_edge, above_edge, fresh, cost
    )
    out = run_last(given, part, mass2, below2, above2)
    return out.reshape(centroids.shape), placed.reshape(count)


def solution(mesh):
    return jax.shard_map(
        per_device,
        mesh=mesh,
        in_specs=(
            P(("own", "rep"), None),
            P(("own", "rep")),
            P(("own", "rep"), None),
            P("own", "rep", None, None),
        ),
        out_specs=(P("own", "rep", None, None), P(("own", "rep"))),
        check_vma=False,
    )
```

```python
import functools
import math

import jax
import jax.numpy as jnp
from jax import lax
from jax.experimental import pallas as pl
from jax.experimental.pallas import tpu as pltpu
from jax.sharding import PartitionSpec as P

PRIOR = 1.0
LOG2E = 1.4426950408889634
LANES = 128
MASS_ROWS = 16
VMEM = pltpu.VMEM
HBM = pltpu.HBM
ANY = pl.ANY
F32 = jnp.float32
BF16 = jnp.bfloat16


def call(kernel, ins, outs, scratch=(), flops=0, limit=24, aliases=None):
    arrays = [x if space is ANY else pltpu.with_memory_space_constraint(x, space) for x, space in ins]
    made = pl.pallas_call(
        kernel,
        in_specs=[pl.BlockSpec(memory_space=space) for _, space in ins],
        out_shape=[space(*x) if space is not ANY else sds(*x) for x, space in outs],
        out_specs=[pl.BlockSpec(memory_space=space) for _, space in outs],
        scratch_shapes=list(scratch),
        input_output_aliases=aliases or {},
        compiler_params=pltpu.CompilerParams(vmem_limit_bytes=limit << 20),
        cost_estimate=pl.CostEstimate(flops=flops, bytes_accessed=1 << 20, transcendentals=0),
    )(*arrays)
    return made[0] if len(outs) == 1 else made


def sds(shape, dtype):
    return jax.ShapeDtypeStruct(shape, dtype)


def matmul(a, b, contract):
    return lax.dot_general(a, b, (contract, ((), ())), preferred_element_type=F32)


def regroup_kernel(pairs, dest_hbm, rows_hbm, out_hbm, dest_ref, rows_ref, wide, out_ref, in_sems, out_sems):
    count, features = rows_ref.shape
    per_pair = count // pairs
    chunks = features // LANES
    fetch_dest = pltpu.make_async_copy(dest_hbm, dest_ref, in_sems.at[0])
    fetch_rows = pltpu.make_async_copy(rows_hbm, rows_ref, in_sems.at[1])
    fetch_dest.start()
    fetch_rows.start()
    fetch_dest.wait()
    dest = dest_ref[...]
    place = lax.rem(dest, per_pair) * pairs + lax.div(dest, count)
    parts = 4
    step = pairs // parts
    span = step * per_pair * chunks
    rows = None
    stores = []
    for part in range(parts):
        first = part * step
        picks = []
        for slot in range(per_pair):
            ids = lax.broadcasted_iota(jnp.int32, (step, count), 0) + (slot * pairs + first)
            picks.append(jnp.where(ids == place, 1.0, 0.0).astype(BF16))
        pick = jnp.concatenate(picks, axis=0)
        if rows is None:
            fetch_rows.wait()
            rows = rows_ref[...]
        moved = matmul(pick, rows, ((1,), (0,)))
        for slot in range(per_pair):
            for f in range(chunks):
                line = (first * chunks + f) * per_pair + slot
                wide[pl.ds(line, step, stride=chunks * per_pair), :] = moved[
                    slot * step : (slot + 1) * step, f * LANES : (f + 1) * LANES
                ]
        here = pl.ds(part * span, span)
        out_ref[here, :] = wide[here, :].astype(BF16)
        store = pltpu.make_async_copy(out_ref.at[here], out_hbm.at[here], out_sems.at[part])
        store.start()
        stores.append(store)
    for store in stores:
        store.wait()


def unpack_rows(lines_ref, rows_ref, wide, pairs):
    count, features = rows_ref.shape
    per_pair = count // pairs
    chunks = features // LANES
    parts = 4
    step = pairs // parts
    span = step * per_pair * chunks
    for part in range(parts):
        here = pl.ds(part * span, span)
        wide[here, :] = lines_ref[here, :].astype(F32)
        for slot in range(per_pair):
            for f in range(chunks):
                got = wide[pl.ds(part * span + f * per_pair + slot, step, stride=chunks * per_pair), :]
                rows_ref[pl.ds(slot * pairs + part * step, step), f * LANES : (f + 1) * LANES] = got.astype(BF16)


STEP = 256


def half_scale(features):
    return 0.5 * LOG2E / math.sqrt(features)


def scored(flat, biases, slots, rows, ids):
    cross = matmul(flat, rows, ((1,), (1,)))
    size = flat.shape[0] // len(slots)
    factor = 2.0 * half_scale(flat.shape[1])
    scores = []
    for k, w in enumerate(slots):
        hit = jnp.max(jnp.where(ids == w, 0.0, -jnp.inf), axis=0, keepdims=True)
        scores.append(cross[k * size : (k + 1) * size] * factor + (hit - biases[k]))
    return scores


def highest(scores):
    return functools.reduce(jnp.maximum, [jnp.max(s, axis=0, keepdims=True) for s in scores])


def added(parts):
    return functools.reduce(jnp.add, [jnp.sum(p, axis=0, keepdims=True) for p in parts])


def square_biases(blocks):
    half = half_scale(blocks[0].shape[1])
    wide = [block.astype(F32) for block in blocks]
    return [jnp.sum(w * w, axis=1, keepdims=True) * half for w in wide]


def row_sums(parts):
    return [jnp.sum(p, axis=1, keepdims=True) for p in parts]


def diagonal(size):
    across = lax.broadcasted_iota(jnp.int32, (size, size), 0)
    return across == lax.broadcasted_iota(jnp.int32, (size, size), 1)


def pack_mass(masses):
    size = masses[0].shape[0]
    eye = diagonal(size)
    row = lax.broadcasted_iota(jnp.int32, (MASS_ROWS, size), 0)
    packed = jnp.zeros((MASS_ROWS, size), F32)
    for k, mass in enumerate(masses):
        line = jnp.sum(jnp.where(eye, mass, 0.0), axis=0, keepdims=True)
        high = line.astype(BF16).astype(F32)
        packed = jnp.where(row == 2 * k, high, jnp.where(row == 2 * k + 1, line - high, packed))
    return packed.astype(BF16)


def unpack_mass(packed, which):
    size = packed.shape[1]
    row = lax.broadcasted_iota(jnp.int32, packed.shape, 0)
    line = jnp.sum(jnp.where(lax.div(row, 2) == which, packed.astype(F32), 0.0), axis=0, keepdims=True)
    return jnp.sum(jnp.where(diagonal(size), line, 0.0), axis=1, keepdims=True)


def package(pkg_ref, sums, masses):
    size, features = sums[0].shape
    blocks = len(sums)
    for f in range(features // LANES):
        for k in range(blocks):
            first = (f * blocks + k) * size
            pkg_ref[first : first + size, :] = sums[k][:, f * LANES : (f + 1) * LANES].astype(BF16)
    pkg_ref[blocks * size * (features // LANES) :, :] = pack_mass(masses)


def unpack(pkg_ref, which, blocks, size):
    chunks = (pkg_ref.shape[0] - MASS_ROWS) // (blocks * size)
    firsts = [(f * blocks + which) * size for f in range(chunks)]
    sums = jnp.concatenate([pkg_ref[first : first + size, :] for first in firsts], axis=1)
    return sums.astype(F32), unpack_mass(pkg_ref[blocks * size * chunks :, :], which)


def package_lines(blocks, size, features):
    return (((blocks * size * (features // LANES) + MASS_ROWS, LANES), BF16), VMEM)


def arrival_kernel(
    pairs, lines_ref, ids_ref, own_ref, rows_ref, weights_ref, top_ref, total_ref, wide
):
    blocks, size, _ = own_ref.shape
    own = [own_ref[k] for k in range(blocks)]
    biases = square_biases(own)
    flat = jnp.concatenate(own, axis=0)
    unpack_rows(lines_ref, rows_ref, wide, pairs)
    for start in range(0, rows_ref.shape[0], STEP):
        here = slice(start, start + STEP)
        scores = scored(flat, biases, range(1, blocks + 1), rows_ref[here, :], ids_ref[:, here])
        top = highest(scores)
        top_ref[:, here] = top
        weights = [jnp.exp2(score - top) for score in scores]
        total_ref[:, here] = added(weights)
        for k in range(blocks):
            weights_ref[k * size : (k + 1) * size, here] = weights[k]


def first_kernel(
    rows_ref, ids_ref, weights_ref, top_ref, total_ref, left_ref, own_ref, right_ref,
    scale_ref, sums_ref, mass_ref, up_ref, down_ref, resp_ref,
):
    count_own, size, _ = own_ref.shape
    last = count_own + 1
    halo = [left_ref[...], right_ref[...]]
    biases = square_biases(halo)
    flat = jnp.concatenate(halo, axis=0)
    edges = (halo[0], own_ref[0], own_ref[count_own - 1], halo[1])
    mass = [0.0] * len(edges)
    for start in range(0, rows_ref.shape[0], STEP):
        here = slice(start, start + STEP)
        scores = scored(flat, biases, (0, last), rows_ref[here, :], ids_ref[:, here])
        top = jnp.maximum(highest(scores), top_ref[:, here])
        shrink = jnp.exp2(top_ref[:, here] - top)
        weights = [jnp.exp2(score - top) for score in scores]
        scale = 1.0 / (added(weights) + shrink * total_ref[:, here])
        own_scale = shrink * scale
        scale_ref[:, here] = own_scale
        resps = (
            weights[0] * scale,
            weights_ref[:size, here] * own_scale,
            weights_ref[(count_own - 1) * size :, here] * own_scale,
            weights[1] * scale,
        )
        for k, resp in enumerate(resps):
            resp_ref[k * size : (k + 1) * size, here] = resp.astype(BF16)
            mass[k] = mass[k] + resp
    mass = row_sums(mass)
    rows = rows_ref[...]
    sums = []
    for k, block in enumerate(edges):
        total = matmul(resp_ref[k * size : (k + 1) * size, :], rows, ((1,), (0,)))
        sums_ref[k] = total + PRIOR * block.astype(F32)
        sums.append(total)
        mass_ref[k * size : (k + 1) * size, :] = mass[k] + PRIOR
    package(up_ref, sums[2:], mass[2:])
    package(down_ref, sums[:2], mass[:2])


def ratio(total, tally):
    return (total * (1.0 / tally)).astype(BF16)


def inner_kernel(
    rows_ref, ids_ref, weights_ref, scale_ref, own_ref, fresh_ref, norm_ref, next_ref, top_ref, total_ref, resp_ref
):
    blocks, size, _ = own_ref.shape
    inner = blocks - 2
    count = rows_ref.shape[0]
    mass = [0.0] * inner
    for start in range(0, count, STEP):
        here = slice(start, start + STEP)
        for k in range(inner):
            there = slice(k * size, (k + 1) * size)
            resp = weights_ref[(k + 1) * size : (k + 2) * size, here] * scale_ref[:, here]
            resp_ref[there, here] = resp.astype(BF16)
            mass[k] = mass[k] + resp
    mass = row_sums(mass)
    rows = rows_ref[...]
    new = []
    for k in range(inner):
        total = matmul(resp_ref[k * size : (k + 1) * size, :], rows, ((1,), (0,)))
        new.append(ratio(total + PRIOR * own_ref[k + 1].astype(F32), mass[k] + PRIOR))
        fresh_ref[k] = new[k]
    biases = square_biases(new)
    flat = jnp.concatenate(new, axis=0)
    for start in range(0, count, STEP):
        here = slice(start, start + STEP)
        scores = scored(flat, biases, range(2, inner + 2), rows_ref[here, :], ids_ref[:, here])
        top = highest(scores)
        top_ref[:, here] = top
        safe = jnp.where(top == -jnp.inf, 0.0, top)
        weights = [jnp.exp2(score - safe) for score in scores]
        total_ref[:, here] = added(weights)
        for k in range(inner):
            next_ref[k * size : (k + 1) * size, here] = weights[k]
    eye = diagonal(LANES)
    for start in range(0, count, LANES):
        wide = rows_ref[start : start + LANES, :].astype(F32)
        norm = jnp.sum(wide * wide, axis=1, keepdims=True)
        norm_ref[:, start : start + LANES] = jnp.sum(jnp.where(eye, norm, 0.0), axis=0, keepdims=True)


def renewed(pkg_ref, sums, masses):
    new = []
    for k in range(2):
        more, tally = unpack(pkg_ref, k, 2, sums[k].shape[0])
        new.append(ratio(sums[k] + more, masses[k] + tally))
    return new


def below_kernel(
    rows_ref, ids_ref, sums_ref, mass_ref, top_ref, total_ref, below_ref,
    edge_ref, weights_ref, new_top_ref, new_total_ref, shrink_ref,
):
    size = sums_ref.shape[1]
    new = renewed(below_ref, [sums_ref[k] for k in range(2)], [mass_ref[k * size : (k + 1) * size, :] for k in range(2)])
    edge_ref[...] = new[1]
    biases = square_biases(new)
    flat = jnp.concatenate(new, axis=0)
    for start in range(0, rows_ref.shape[0], STEP):
        here = slice(start, start + STEP)
        scores = scored(flat, biases, (0, 1), rows_ref[here, :], ids_ref[:, here])
        before = top_ref[:, here]
        top = jnp.maximum(highest(scores), before)
        safe = jnp.where(top == -jnp.inf, 0.0, top)
        shrink = jnp.exp2(before - safe)
        weights = [jnp.exp2(score - safe) for score in scores]
        new_top_ref[:, here] = top
        shrink_ref[:, here] = shrink
        new_total_ref[:, here] = added(weights) + shrink * total_ref[:, here]
        for k in range(2):
            weights_ref[k * size : (k + 1) * size, here] = weights[k]


def above_kernel(
    rows_ref, ids_ref, sums_ref, mass_ref, norm_ref, top_ref, total_ref, shrink_ref, weights_ref, above_ref,
    edge_ref, outer_ref, above_scale_ref, below_scale_ref, inner_scale_ref, cost_ref, up_ref, down_ref, resp_ref,
):
    size = sums_ref.shape[1]
    last = 5
    new = renewed(
        above_ref, [sums_ref[k] for k in range(2, 4)], [mass_ref[k * size : (k + 1) * size, :] for k in range(2, 4)]
    )
    edge_ref[...] = new[0]
    biases = square_biases(new)
    flat = jnp.concatenate(new, axis=0)
    mass = [0.0, 0.0]
    half = 0.5 / math.sqrt(rows_ref.shape[1])
    for start in range(0, rows_ref.shape[0], STEP):
        here = slice(start, start + STEP)
        scores = scored(flat, biases, (last - 1, last), rows_ref[here, :], ids_ref[:, here])
        before = top_ref[:, here]
        top = jnp.maximum(highest(scores), before)
        fade = jnp.exp2(before - top)
        weights = [jnp.exp2(score - top) for score in scores]
        total = added(weights) + fade * total_ref[:, here]
        scale = 1.0 / total
        below_scale = scale * fade
        above_scale_ref[:, here] = scale
        below_scale_ref[:, here] = below_scale
        inner_scale_ref[:, here] = below_scale * shrink_ref[:, here]
        cost_ref[:, here] = norm_ref[:, here] * half - (top * (1.0 / LOG2E) + jnp.log(total))
        outer_ref[:, here] = weights[0]
        for k, resp in enumerate((weights_ref[:size, here] * below_scale, weights[1] * scale)):
            resp_ref[k * size : (k + 1) * size, here] = resp.astype(BF16)
            mass[k] = mass[k] + resp
    mass = row_sums(mass)
    rows = rows_ref[...]
    for k, pkg in enumerate((down_ref, up_ref)):
        total = matmul(resp_ref[k * size : (k + 1) * size, :], rows, ((1,), (0,)))
        package(pkg, [total], [mass[k]])


def interleave(lines_ref, out_ref, slots):
    count = lines_ref.shape[1]
    pairs = count // slots
    width = LANES * slots
    groups = pairs // LANES
    row = lax.broadcasted_iota(jnp.int32, (width, width), 0)
    lane = lax.broadcasted_iota(jnp.int32, (width, width), 1)
    pick = jnp.where(row == lax.rem(lane, slots) * LANES + lax.div(lane, slots), 1.0, 0.0).astype(BF16)
    pieces = []
    for g in range(groups):
        cuts = [lines_ref[:, s * pairs + g * LANES : s * pairs + (g + 1) * LANES] for s in range(slots)]
        left = jnp.concatenate(cuts, axis=1)
        for _ in range(3):
            piece = left.astype(BF16).astype(F32)
            pieces.append(piece)
            left = left - piece
    pieces += [jnp.zeros_like(pieces[0])] * (-len(pieces) % 16)
    moved = matmul(jnp.concatenate(pieces, axis=0).astype(BF16), pick, ((1,), (0,)))
    for g in range(groups):
        line = moved[3 * g : 3 * g + 1] + moved[3 * g + 1 : 3 * g + 2] + moved[3 * g + 2 : 3 * g + 3]
        for s in range(slots):
            out_ref[g * slots + s : g * slots + s + 1, :] = line[:, s * LANES : (s + 1) * LANES]


def own_kernel(
    slots, rows_ref, inner_ref, inner_scale_ref, below_ref, below_scale_ref, above_ref, above_scale_ref,
    below_edge_ref, above_edge_ref, fresh_ref, cost_ref,
    out_hbm, part_ref, mass_ref, placed_ref, done_ref, resp_ref, sem,
):
    inner, size, _ = fresh_ref.shape
    rows = rows_ref[...]

    def summed(weights):
        mass = [0.0] * len(weights)
        for start in range(0, rows_ref.shape[0], STEP):
            here = slice(start, start + STEP)
            for k, (ref, first, by_ref) in enumerate(weights):
                resp = ref[first : first + size, here] * by_ref[:, here]
                resp_ref[k * size : (k + 1) * size, here] = resp.astype(BF16)
                mass[k] = mass[k] + resp
        sums = [
            matmul(resp_ref[k * size : (k + 1) * size, :], rows, ((1,), (0,))) for k in range(len(weights))
        ]
        return sums, row_sums(mass)

    sums, mass = summed([(inner_ref, k * size, inner_scale_ref) for k in range(inner)])
    for k in range(inner):
        done_ref[k] = ratio(sums[k] + PRIOR * fresh_ref[k].astype(F32), mass[k] + PRIOR)
    store = pltpu.make_async_copy(done_ref, out_hbm.at[pl.ds(1, inner)], sem)
    store.start()
    sums, mass = summed([(below_ref, size, below_scale_ref), (above_ref, 0, above_scale_ref)])
    for k, edge_ref in enumerate((below_edge_ref, above_edge_ref)):
        part_ref[k] = sums[k] + PRIOR * edge_ref[...].astype(F32)
        mass_ref[k * size : (k + 1) * size, :] = mass[k] + PRIOR
    interleave(cost_ref, placed_ref, slots)
    store.wait()


def last_kernel(given_hbm, part_ref, mass_ref, below_ref, above_ref, out_hbm, done_ref, sems):
    blocks, size, _ = out_hbm.shape
    stores = []
    for e, (k, pkg) in enumerate(((0, below_ref), (blocks - 1, above_ref))):
        more, tally = unpack(pkg, 0, 1, size)
        done_ref[e] = ratio(part_ref[e] + more, mass_ref[e * size : (e + 1) * size, :] + tally)
        stores.append(pltpu.make_async_copy(done_ref.at[e], out_hbm.at[k], sems.at[e]))
        stores[-1].start()
    for store in stores:
        store.wait()


def wide_lines(lines, stride):
    return pltpu.VMEM((lines + stride + 4, LANES), F32)


def run_regroup(pairs, dest, rows):
    count, features = rows.shape
    lines = count * features // LANES
    dma = pltpu.SemaphoreType.DMA
    return call(
        functools.partial(regroup_kernel, pairs),
        [(dest, HBM), (rows, HBM)],
        [(((lines, LANES), BF16), HBM)],
        [
            VMEM((1, count), jnp.int32),
            VMEM((count, features), BF16),
            wide_lines(lines, lines // pairs),
            VMEM((lines, LANES), BF16),
            dma((2,)),
            dma((4,)),
        ],
        2 * count * features * count,
    )


def run_arrival(pairs, arrived, ids, own):
    lines, count = arrived.shape[0], ids.shape[1]
    blocks, size, features = own.shape
    line = (((1, count), F32), VMEM)
    return call(
        functools.partial(arrival_kernel, pairs),
        [(arrived, VMEM), (ids, VMEM), (own, VMEM)],
        [(((count, features), BF16), VMEM), (((blocks * size, count), F32), VMEM), line, line],
        [wide_lines(lines, lines // pairs)],
        2 * count * features * blocks * size,
    )


def run_first(rows, ids, weights, top, total, left, own, right):
    blocks, size, features = own.shape
    count = rows.shape[0]
    two = package_lines(2, size, features)
    return call(
        first_kernel,
        [(x, VMEM) for x in (rows, ids, weights, top, total, left, own, right)],
        [(((1, count), F32), VMEM), (((4, size, features), F32), VMEM), (((4 * size, 1), F32), VMEM), two, two],
        [VMEM((4 * size, count), BF16)],
        2 * count * features * 6 * size,
    )


def run_inner(rows, ids, weights, scale, own):
    blocks, size, features = own.shape
    count = rows.shape[0]
    inner = (blocks - 2) * size
    line = (((1, count), F32), VMEM)
    return call(
        inner_kernel,
        [(x, VMEM) for x in (rows, ids, weights, scale, own)],
        [(((blocks - 2, size, features), BF16), VMEM), line, (((inner, count), F32), VMEM), line, line],
        [VMEM((inner, count), BF16)],
        2 * count * features * 4 * size,
    )


def run_below(rows, ids, sums, mass, top, total, below):
    _, size, features = sums.shape
    count = rows.shape[0]
    line = (((1, count), F32), VMEM)
    return call(
        below_kernel,
        [(x, VMEM) for x in (rows, ids, sums, mass, top, total, below)],
        [(((size, features), BF16), VMEM), (((2 * size, count), F32), VMEM), line, line, line],
        flops=2 * count * features * 2 * size,
    )


def run_above(rows, ids, sums, mass, norm, top, total, shrink, weights, above):
    _, size, features = sums.shape
    count = rows.shape[0]
    line = (((1, count), F32), VMEM)
    one = package_lines(1, size, features)
    return call(
        above_kernel,
        [(x, VMEM) for x in (rows, ids, sums, mass, norm, top, total, shrink, weights, above)],
        [(((size, features), BF16), VMEM), (((size, count), F32), VMEM), line, line, line, line, one, one],
        [VMEM((2 * size, count), BF16)],
        2 * count * features * 4 * size,
    )


def run_own(slots, rows, inner, inner_scale, below, below_scale, above, above_scale, below_edge, above_edge, fresh, cost):
    blocks, size, features = fresh.shape[0] + 2, fresh.shape[1], fresh.shape[2]
    count = rows.shape[0]
    ins = (rows, inner, inner_scale, below, below_scale, above, above_scale, below_edge, above_edge, fresh, cost)
    return call(
        functools.partial(own_kernel, slots),
        [(x, VMEM) for x in ins],
        [
            (((blocks, size, features), BF16), HBM),
            (((2, size, features), F32), VMEM),
            (((2 * size, 1), F32), VMEM),
            (((count // LANES, LANES), F32), VMEM),
        ],
        [VMEM((blocks - 2, size, features), BF16), VMEM((2 * size, count), BF16), pltpu.SemaphoreType.DMA],
        2 * count * features * blocks * size,
    )


def run_last(given, part, mass, below, above):
    return call(
        last_kernel,
        [(given, HBM)] + [(x, VMEM) for x in (part, mass, below, above)],
        [((given.shape, BF16), HBM)],
        [VMEM(part.shape, BF16), pltpu.SemaphoreType.DMA((2,))],
        aliases={0: 0},
    )


def swap(up, down, axis):
    devices = lax.axis_size(axis)
    pairs = [(i, i + 1) for i in range(devices - 1)]
    below = lax.ppermute(up, axis, pairs)
    above = lax.ppermute(down, axis, [(j, i) for i, j in pairs])
    return below, above


def per_device(sample_rows, destination, neighbours, centroids):
    own_count, rep_count = lax.axis_size("own"), lax.axis_size("rep")
    pairs = own_count * rep_count
    count, features = sample_rows.shape
    per_pair = count // pairs
    chunks = features // LANES
    lines = count * chunks
    blocks, _, size, _ = centroids.shape
    own = centroids.reshape(blocks, size, features)
    outgoing = run_regroup(pairs, destination.reshape(1, count), sample_rows)
    left, right = swap(own[blocks - 1], own[0], "own")
    first_block = lax.axis_index("own") * blocks - 1
    ids = (neighbours // rep_count - first_block).T
    ids = ids.reshape(-1, pairs, per_pair).swapaxes(1, 2).reshape(-1, count)
    arrived = lax.all_to_all(
        outgoing.reshape(pairs, lines // pairs // 4, 4, LANES), ("own", "rep"), split_axis=0, concat_axis=0, tiled=True
    ).reshape(lines, LANES)

    rows, weights1, top1, total1 = run_arrival(pairs, arrived, ids, own)
    scale1, sums1, mass1, up1, down1 = run_first(rows, ids, weights1, top1, total1, left, own, right)
    below1, above1 = swap(up1, down1, "own")
    fresh, norm, inner2, top, total = run_inner(rows, ids, weights1, scale1, own)
    below_edge, below_w, top, total, shrink = run_below(rows, ids, sums1, mass1, top, total, below1)
    above_edge, above_w, above_by, below_by, inner_by, cost, up2, down2 = run_above(
        rows, ids, sums1, mass1, norm, top, total, shrink, below_w, above1
    )
    below2, above2 = swap(up2, down2, "own")
    given, part, mass2, placed = run_own(
        per_pair, rows, inner2, inner_by, below_w, below_by, above_w, above_by, below_edge, above_edge, fresh, cost
    )
    out = run_last(given, part, mass2, below2, above2)
    return out.reshape(centroids.shape), placed.reshape(count)


def solution(mesh):
    return jax.shard_map(
        per_device,
        mesh=mesh,
        in_specs=(
            P(("own", "rep"), None),
            P(("own", "rep")),
            P(("own", "rep"), None),
            P("own", "rep", None, None),
        ),
        out_specs=(P("own", "rep", None, None), P(("own", "rep"))),
        check_vma=False,
    )
```

```python
import functools
import math

import jax
import jax.numpy as jnp
from jax import lax
from jax.experimental import pallas as pl
from jax.experimental.pallas import tpu as pltpu
from jax.sharding import PartitionSpec as P

PRIOR = 1.0
LOG2E = 1.4426950408889634
LANES = 128
MASS_ROWS = 16
VMEM = pltpu.VMEM
HBM = pltpu.HBM
ANY = pl.ANY
F32 = jnp.float32
BF16 = jnp.bfloat16


def call(kernel, ins, outs, scratch=(), flops=0, limit=24, aliases=None):
    arrays = [x if space is ANY else pltpu.with_memory_space_constraint(x, space) for x, space in ins]
    made = pl.pallas_call(
        kernel,
        in_specs=[pl.BlockSpec(memory_space=space) for _, space in ins],
        out_shape=[space(*x) if space is not ANY else sds(*x) for x, space in outs],
        out_specs=[pl.BlockSpec(memory_space=space) for _, space in outs],
        scratch_shapes=list(scratch),
        input_output_aliases=aliases or {},
        compiler_params=pltpu.CompilerParams(vmem_limit_bytes=limit << 20),
        cost_estimate=pl.CostEstimate(flops=flops, bytes_accessed=1 << 20, transcendentals=0),
    )(*arrays)
    return made[0] if len(outs) == 1 else made


def sds(shape, dtype):
    return jax.ShapeDtypeStruct(shape, dtype)


def matmul(a, b, contract):
    return lax.dot_general(a, b, (contract, ((), ())), preferred_element_type=F32)


def regroup_kernel(pairs, dest_hbm, rows_hbm, out_hbm, dest_ref, rows_ref, wide, out_ref, in_sems, out_sems):
    count, features = rows_ref.shape
    per_pair = count // pairs
    chunks = features // LANES
    fetch_dest = pltpu.make_async_copy(dest_hbm, dest_ref, in_sems.at[0])
    fetch_rows = pltpu.make_async_copy(rows_hbm, rows_ref, in_sems.at[1])
    fetch_dest.start()
    fetch_rows.start()
    fetch_dest.wait()
    dest = dest_ref[...]
    place = lax.rem(dest, per_pair) * pairs + lax.div(dest, count)
    parts = 4
    step = pairs // parts
    span = step * per_pair * chunks
    rows = None
    stores = []
    for part in range(parts):
        first = part * step
        picks = []
        for slot in range(per_pair):
            ids = lax.broadcasted_iota(jnp.int32, (step, count), 0) + (slot * pairs + first)
            picks.append(jnp.where(ids == place, 1.0, 0.0).astype(BF16))
        pick = jnp.concatenate(picks, axis=0)
        if rows is None:
            fetch_rows.wait()
            rows = rows_ref[...]
        moved = matmul(pick, rows, ((1,), (0,)))
        for slot in range(per_pair):
            for f in range(chunks):
                line = (first * chunks + f) * per_pair + slot
                wide[pl.ds(line, step, stride=chunks * per_pair), :] = moved[
                    slot * step : (slot + 1) * step, f * LANES : (f + 1) * LANES
                ]
        here = pl.ds(part * span, span)
        out_ref[here, :] = wide[here, :].astype(BF16)
        store = pltpu.make_async_copy(out_ref.at[here], out_hbm.at[here], out_sems.at[part])
        store.start()
        stores.append(store)
    for store in stores:
        store.wait()


def unpack_rows(lines_ref, rows_ref, wide, pairs):
    count, features = rows_ref.shape
    per_pair = count // pairs
    chunks = features // LANES
    parts = 4
    step = pairs // parts
    span = step * per_pair * chunks
    for part in range(parts):
        here = pl.ds(part * span, span)
        wide[here, :] = lines_ref[here, :].astype(F32)
        for slot in range(per_pair):
            for f in range(chunks):
                got = wide[pl.ds(part * span + f * per_pair + slot, step, stride=chunks * per_pair), :]
                rows_ref[pl.ds(slot * pairs + part * step, step), f * LANES : (f + 1) * LANES] = got.astype(BF16)


STEP = 512


def half_scale(features):
    return 0.5 * LOG2E / math.sqrt(features)


def scored(flat, biases, slots, rows, hits):
    cross = matmul(flat, rows, ((1,), (1,)))
    size = flat.shape[0] // len(slots)
    factor = 2.0 * half_scale(flat.shape[1])
    scores = []
    for k, w in enumerate(slots):
        hit = hits[w : w + 1, :]
        scores.append(cross[k * size : (k + 1) * size] * factor + (hit - biases[k]))
    return scores


def highest(scores):
    return functools.reduce(jnp.maximum, [jnp.max(s, axis=0, keepdims=True) for s in scores])


def added(parts):
    return functools.reduce(jnp.add, [jnp.sum(p, axis=0, keepdims=True) for p in parts])


def square_biases(blocks):
    half = half_scale(blocks[0].shape[1])
    wide = [block.astype(F32) for block in blocks]
    return [jnp.sum(w * w, axis=1, keepdims=True) * half for w in wide]


def row_sums(parts):
    return [jnp.sum(p, axis=1, keepdims=True) for p in parts]


def diagonal(size):
    across = lax.broadcasted_iota(jnp.int32, (size, size), 0)
    return across == lax.broadcasted_iota(jnp.int32, (size, size), 1)


def pack_mass(masses):
    size = masses[0].shape[0]
    eye = diagonal(size)
    row = lax.broadcasted_iota(jnp.int32, (MASS_ROWS, size), 0)
    packed = jnp.zeros((MASS_ROWS, size), F32)
    for k, mass in enumerate(masses):
        line = jnp.sum(jnp.where(eye, mass, 0.0), axis=0, keepdims=True)
        high = line.astype(BF16).astype(F32)
        packed = jnp.where(row == 2 * k, high, jnp.where(row == 2 * k + 1, line - high, packed))
    return packed.astype(BF16)


def unpack_mass(packed, which):
    size = packed.shape[1]
    row = lax.broadcasted_iota(jnp.int32, packed.shape, 0)
    line = jnp.sum(jnp.where(lax.div(row, 2) == which, packed.astype(F32), 0.0), axis=0, keepdims=True)
    return jnp.sum(jnp.where(diagonal(size), line, 0.0), axis=1, keepdims=True)


def package(pkg_ref, sums, masses):
    size, features = sums[0].shape
    blocks = len(sums)
    for f in range(features // LANES):
        for k in range(blocks):
            first = (f * blocks + k) * size
            pkg_ref[first : first + size, :] = sums[k][:, f * LANES : (f + 1) * LANES].astype(BF16)
    pkg_ref[blocks * size * (features // LANES) :, :] = pack_mass(masses)


def unpack(pkg_ref, which, blocks, size):
    chunks = (pkg_ref.shape[0] - MASS_ROWS) // (blocks * size)
    firsts = [(f * blocks + which) * size for f in range(chunks)]
    sums = jnp.concatenate([pkg_ref[first : first + size, :] for first in firsts], axis=1)
    return sums.astype(F32), unpack_mass(pkg_ref[blocks * size * chunks :, :], which)


def package_lines(blocks, size, features):
    return (((blocks * size * (features // LANES) + MASS_ROWS, LANES), BF16), VMEM)


def prepare_kernel(ids_ref, own_ref, hits_ref, bias_ref):
    ids = ids_ref[...]
    hits_ref[...] = jnp.full(hits_ref.shape, -jnp.inf, F32)
    blocks, size, _ = own_ref.shape
    for w in range(blocks + 2):
        hits_ref[w : w + 1, :] = jnp.max(jnp.where(ids == w, 0.0, -jnp.inf), axis=0, keepdims=True)
    for k, bias in enumerate(square_biases([own_ref[k] for k in range(blocks)])):
        bias_ref[k * size : (k + 1) * size, :] = bias


def arrival_kernel(
    pairs, lines_ref, hits_ref, own_ref, bias_ref, rows_ref, weights_ref, top_ref, total_ref, wide
):
    blocks, size, _ = own_ref.shape
    own = [own_ref[k] for k in range(blocks)]
    biases = [bias_ref[k * size : (k + 1) * size, :] for k in range(blocks)]
    flat = jnp.concatenate(own, axis=0)
    unpack_rows(lines_ref, rows_ref, wide, pairs)
    for start in range(0, rows_ref.shape[0], STEP):
        here = slice(start, start + STEP)
        scores = scored(flat, biases, range(1, blocks + 1), rows_ref[here, :], hits_ref[:, here])
        top = highest(scores)
        top_ref[:, here] = top
        weights = [jnp.exp2(score - top) for score in scores]
        total_ref[:, here] = added(weights)
        for k in range(blocks):
            weights_ref[k * size : (k + 1) * size, here] = weights[k]


def first_kernel(
    rows_ref, hits_ref, weights_ref, top_ref, total_ref, left_ref, own_ref, right_ref,
    scale_ref, sums_ref, mass_ref, up_ref, down_ref, resp_ref,
):
    count_own, size, _ = own_ref.shape
    last = count_own + 1
    halo = [left_ref[...], right_ref[...]]
    biases = square_biases(halo)
    flat = jnp.concatenate(halo, axis=0)
    edges = (halo[0], own_ref[0], own_ref[count_own - 1], halo[1])
    mass = [0.0] * len(edges)
    for start in range(0, rows_ref.shape[0], STEP):
        here = slice(start, start + STEP)
        scores = scored(flat, biases, (0, last), rows_ref[here, :], hits_ref[:, here])
        top = jnp.maximum(highest(scores), top_ref[:, here])
        shrink = jnp.exp2(top_ref[:, here] - top)
        weights = [jnp.exp2(score - top) for score in scores]
        scale = 1.0 / (added(weights) + shrink * total_ref[:, here])
        own_scale = shrink * scale
        scale_ref[:, here] = own_scale
        resps = (
            weights[0] * scale,
            weights_ref[:size, here] * own_scale,
            weights_ref[(count_own - 1) * size :, here] * own_scale,
            weights[1] * scale,
        )
        for k, resp in enumerate(resps):
            resp_ref[k * size : (k + 1) * size, here] = resp.astype(BF16)
            mass[k] = mass[k] + resp
    mass = row_sums(mass)
    rows = rows_ref[...]
    sums = []
    for k, block in enumerate(edges):
        total = matmul(resp_ref[k * size : (k + 1) * size, :], rows, ((1,), (0,)))
        sums_ref[k] = total + PRIOR * block.astype(F32)
        sums.append(total)
        mass_ref[k * size : (k + 1) * size, :] = mass[k] + PRIOR
    package(up_ref, sums[2:], mass[2:])
    package(down_ref, sums[:2], mass[:2])


def ratio(total, tally):
    return (total * (1.0 / tally)).astype(BF16)


def inner_kernel(
    rows_ref, hits_ref, weights_ref, scale_ref, own_ref, fresh_ref, norm_ref, next_ref, top_ref, total_ref, resp_ref
):
    blocks, size, _ = own_ref.shape
    inner = blocks - 2
    count = rows_ref.shape[0]
    mass = [0.0] * inner
    for start in range(0, count, STEP):
        here = slice(start, start + STEP)
        for k in range(inner):
            there = slice(k * size, (k + 1) * size)
            resp = weights_ref[(k + 1) * size : (k + 2) * size, here] * scale_ref[:, here]
            resp_ref[there, here] = resp.astype(BF16)
            mass[k] = mass[k] + resp
    mass = row_sums(mass)
    rows = rows_ref[...]
    new = []
    for k in range(inner):
        total = matmul(resp_ref[k * size : (k + 1) * size, :], rows, ((1,), (0,)))
        new.append(ratio(total + PRIOR * own_ref[k + 1].astype(F32), mass[k] + PRIOR))
        fresh_ref[k] = new[k]
    biases = square_biases(new)
    flat = jnp.concatenate(new, axis=0)
    for start in range(0, count, STEP):
        here = slice(start, start + STEP)
        scores = scored(flat, biases, range(2, inner + 2), rows_ref[here, :], hits_ref[:, here])
        top = highest(scores)
        top_ref[:, here] = top
        safe = jnp.where(top == -jnp.inf, 0.0, top)
        weights = [jnp.exp2(score - safe) for score in scores]
        total_ref[:, here] = added(weights)
        for k in range(inner):
            next_ref[k * size : (k + 1) * size, here] = weights[k]
    eye = diagonal(LANES)
    for start in range(0, count, LANES):
        wide = rows_ref[start : start + LANES, :].astype(F32)
        norm = jnp.sum(wide * wide, axis=1, keepdims=True)
        norm_ref[:, start : start + LANES] = jnp.sum(jnp.where(eye, norm, 0.0), axis=0, keepdims=True)


def renewed(pkg_ref, sums, masses):
    new = []
    for k in range(2):
        more, tally = unpack(pkg_ref, k, 2, sums[k].shape[0])
        new.append(ratio(sums[k] + more, masses[k] + tally))
    return new


def below_kernel(
    rows_ref, hits_ref, sums_ref, mass_ref, top_ref, total_ref, below_ref,
    edge_ref, weights_ref, new_top_ref, new_total_ref, shrink_ref,
):
    size = sums_ref.shape[1]
    new = renewed(below_ref, [sums_ref[k] for k in range(2)], [mass_ref[k * size : (k + 1) * size, :] for k in range(2)])
    edge_ref[...] = new[1]
    biases = square_biases(new)
    flat = jnp.concatenate(new, axis=0)
    for start in range(0, rows_ref.shape[0], STEP):
        here = slice(start, start + STEP)
        scores = scored(flat, biases, (0, 1), rows_ref[here, :], hits_ref[:, here])
        before = top_ref[:, here]
        top = jnp.maximum(highest(scores), before)
        safe = jnp.where(top == -jnp.inf, 0.0, top)
        shrink = jnp.exp2(before - safe)
        weights = [jnp.exp2(score - safe) for score in scores]
        new_top_ref[:, here] = top
        shrink_ref[:, here] = shrink
        new_total_ref[:, here] = added(weights) + shrink * total_ref[:, here]
        for k in range(2):
            weights_ref[k * size : (k + 1) * size, here] = weights[k]


def above_kernel(
    rows_ref, hits_ref, sums_ref, mass_ref, norm_ref, top_ref, total_ref, shrink_ref, weights_ref, above_ref,
    edge_ref, outer_ref, above_scale_ref, below_scale_ref, inner_scale_ref, cost_ref, up_ref, down_ref, resp_ref,
):
    size = sums_ref.shape[1]
    last = 5
    new = renewed(
        above_ref, [sums_ref[k] for k in range(2, 4)], [mass_ref[k * size : (k + 1) * size, :] for k in range(2, 4)]
    )
    edge_ref[...] = new[0]
    biases = square_biases(new)
    flat = jnp.concatenate(new, axis=0)
    mass = [0.0, 0.0]
    half = 0.5 / math.sqrt(rows_ref.shape[1])
    for start in range(0, rows_ref.shape[0], STEP):
        here = slice(start, start + STEP)
        scores = scored(flat, biases, (last - 1, last), rows_ref[here, :], hits_ref[:, here])
        before = top_ref[:, here]
        top = jnp.maximum(highest(scores), before)
        fade = jnp.exp2(before - top)
        weights = [jnp.exp2(score - top) for score in scores]
        total = added(weights) + fade * total_ref[:, here]
        scale = 1.0 / total
        below_scale = scale * fade
        above_scale_ref[:, here] = scale
        below_scale_ref[:, here] = below_scale
        inner_scale_ref[:, here] = below_scale * shrink_ref[:, here]
        cost_ref[:, here] = norm_ref[:, here] * half - (top * (1.0 / LOG2E) + jnp.log(total))
        outer_ref[:, here] = weights[0]
        for k, resp in enumerate((weights_ref[:size, here] * below_scale, weights[1] * scale)):
            resp_ref[k * size : (k + 1) * size, here] = resp.astype(BF16)
            mass[k] = mass[k] + resp
    mass = row_sums(mass)
    rows = rows_ref[...]
    for k, pkg in enumerate((down_ref, up_ref)):
        total = matmul(resp_ref[k * size : (k + 1) * size, :], rows, ((1,), (0,)))
        package(pkg, [total], [mass[k]])


def interleave(lines_ref, out_ref, slots):
    count = lines_ref.shape[1]
    pairs = count // slots
    width = LANES * slots
    groups = pairs // LANES
    row = lax.broadcasted_iota(jnp.int32, (width, width), 0)
    lane = lax.broadcasted_iota(jnp.int32, (width, width), 1)
    pick = jnp.where(row == lax.rem(lane, slots) * LANES + lax.div(lane, slots), 1.0, 0.0).astype(BF16)
    pieces = []
    for g in range(groups):
        cuts = [lines_ref[:, s * pairs + g * LANES : s * pairs + (g + 1) * LANES] for s in range(slots)]
        left = jnp.concatenate(cuts, axis=1)
        for _ in range(3):
            piece = left.astype(BF16).astype(F32)
            pieces.append(piece)
            left = left - piece
    pieces += [jnp.zeros_like(pieces[0])] * (-len(pieces) % 16)
    moved = matmul(jnp.concatenate(pieces, axis=0).astype(BF16), pick, ((1,), (0,)))
    for g in range(groups):
        line = moved[3 * g : 3 * g + 1] + moved[3 * g + 1 : 3 * g + 2] + moved[3 * g + 2 : 3 * g + 3]
        for s in range(slots):
            out_ref[g * slots + s : g * slots + s + 1, :] = line[:, s * LANES : (s + 1) * LANES]


def own_kernel(
    slots, rows_ref, inner_ref, inner_scale_ref, below_ref, below_scale_ref, above_ref, above_scale_ref,
    below_edge_ref, above_edge_ref, fresh_ref, cost_ref,
    out_hbm, part_ref, mass_ref, placed_hbm, done_ref, resp_ref, placed_ref, sems,
):
    inner, size, _ = fresh_ref.shape
    rows = rows_ref[...]

    def summed(weights):
        mass = [0.0] * len(weights)
        for start in range(0, rows_ref.shape[0], STEP):
            here = slice(start, start + STEP)
            for k, (ref, first, by_ref) in enumerate(weights):
                resp = ref[first : first + size, here] * by_ref[:, here]
                resp_ref[k * size : (k + 1) * size, here] = resp.astype(BF16)
                mass[k] = mass[k] + resp
        sums = [
            matmul(resp_ref[k * size : (k + 1) * size, :], rows, ((1,), (0,))) for k in range(len(weights))
        ]
        return sums, row_sums(mass)

    sums, mass = summed([(inner_ref, k * size, inner_scale_ref) for k in range(inner)])
    for k in range(inner):
        done_ref[k] = ratio(sums[k] + PRIOR * fresh_ref[k].astype(F32), mass[k] + PRIOR)
    store = pltpu.make_async_copy(done_ref, out_hbm.at[pl.ds(1, inner)], sems.at[0])
    store.start()
    interleave(cost_ref, placed_ref, slots)
    place = pltpu.make_async_copy(placed_ref, placed_hbm, sems.at[1])
    place.start()
    sums, mass = summed([(below_ref, size, below_scale_ref), (above_ref, 0, above_scale_ref)])
    for k, edge_ref in enumerate((below_edge_ref, above_edge_ref)):
        part_ref[k] = sums[k] + PRIOR * edge_ref[...].astype(F32)
        mass_ref[k * size : (k + 1) * size, :] = mass[k] + PRIOR
    store.wait()
    place.wait()


def last_kernel(given_hbm, part_ref, mass_ref, below_ref, above_ref, out_hbm, done_ref, sems):
    blocks, size, _ = out_hbm.shape
    stores = []
    for e, (k, pkg) in enumerate(((0, below_ref), (blocks - 1, above_ref))):
        more, tally = unpack(pkg, 0, 1, size)
        done_ref[e] = ratio(part_ref[e] + more, mass_ref[e * size : (e + 1) * size, :] + tally)
        stores.append(pltpu.make_async_copy(done_ref.at[e], out_hbm.at[k], sems.at[e]))
        stores[-1].start()
    for store in stores:
        store.wait()


def wide_lines(lines, stride):
    return pltpu.VMEM((lines + stride + 4, LANES), F32)


def run_regroup(pairs, dest, rows):
    count, features = rows.shape
    lines = count * features // LANES
    dma = pltpu.SemaphoreType.DMA
    return call(
        functools.partial(regroup_kernel, pairs),
        [(dest, HBM), (rows, HBM)],
        [(((lines, LANES), BF16), HBM)],
        [
            VMEM((1, count), jnp.int32),
            VMEM((count, features), BF16),
            wide_lines(lines, lines // pairs),
            VMEM((lines, LANES), BF16),
            dma((2,)),
            dma((4,)),
        ],
        2 * count * features * count,
    )


def run_prepare(ids, own):
    blocks, size, _ = own.shape
    outs = [(((8, ids.shape[1]), F32), VMEM), (((blocks * size, 1), F32), VMEM)]
    return call(prepare_kernel, [(ids, VMEM), (own, VMEM)], outs)


def run_arrival(pairs, arrived, ids, own, bias):
    lines, count = arrived.shape[0], ids.shape[1]
    blocks, size, features = own.shape
    line = (((1, count), F32), VMEM)
    return call(
        functools.partial(arrival_kernel, pairs),
        [(arrived, VMEM), (ids, VMEM), (own, VMEM), (bias, VMEM)],
        [(((count, features), BF16), VMEM), (((blocks * size, count), F32), VMEM), line, line],
        [wide_lines(lines, lines // pairs)],
        2 * count * features * blocks * size,
    )


def run_first(rows, ids, weights, top, total, left, own, right):
    blocks, size, features = own.shape
    count = rows.shape[0]
    two = package_lines(2, size, features)
    return call(
        first_kernel,
        [(x, VMEM) for x in (rows, ids, weights, top, total, left, own, right)],
        [(((1, count), F32), VMEM), (((4, size, features), F32), VMEM), (((4 * size, 1), F32), VMEM), two, two],
        [VMEM((4 * size, count), BF16)],
        2 * count * features * 6 * size,
    )


def run_inner(rows, ids, weights, scale, own):
    blocks, size, features = own.shape
    count = rows.shape[0]
    inner = (blocks - 2) * size
    line = (((1, count), F32), VMEM)
    return call(
        inner_kernel,
        [(x, VMEM) for x in (rows, ids, weights, scale, own)],
        [(((blocks - 2, size, features), BF16), VMEM), line, (((inner, count), F32), VMEM), line, line],
        [VMEM((inner, count), BF16)],
        2 * count * features * 4 * size,
    )


def run_below(rows, ids, sums, mass, top, total, below):
    _, size, features = sums.shape
    count = rows.shape[0]
    line = (((1, count), F32), VMEM)
    return call(
        below_kernel,
        [(x, VMEM) for x in (rows, ids, sums, mass, top, total, below)],
        [(((size, features), BF16), VMEM), (((2 * size, count), F32), VMEM), line, line, line],
        flops=2 * count * features * 2 * size,
    )


def run_above(rows, ids, sums, mass, norm, top, total, shrink, weights, above):
    _, size, features = sums.shape
    count = rows.shape[0]
    line = (((1, count), F32), VMEM)
    one = package_lines(1, size, features)
    return call(
        above_kernel,
        [(x, VMEM) for x in (rows, ids, sums, mass, norm, top, total, shrink, weights, above)],
        [(((size, features), BF16), VMEM), (((size, count), F32), VMEM), line, line, line, line, one, one],
        [VMEM((2 * size, count), BF16)],
        2 * count * features * 4 * size,
    )


def run_own(slots, rows, inner, inner_scale, below, below_scale, above, above_scale, below_edge, above_edge, fresh, cost):
    blocks, size, features = fresh.shape[0] + 2, fresh.shape[1], fresh.shape[2]
    count = rows.shape[0]
    ins = (rows, inner, inner_scale, below, below_scale, above, above_scale, below_edge, above_edge, fresh, cost)
    return call(
        functools.partial(own_kernel, slots),
        [(x, VMEM) for x in ins],
        [
            (((blocks, size, features), BF16), HBM),
            (((2, size, features), F32), VMEM),
            (((2 * size, 1), F32), VMEM),
            (((count // LANES, LANES), F32), HBM),
        ],
        [
            VMEM((blocks - 2, size, features), BF16),
            VMEM((2 * size, count), BF16),
            VMEM((count // LANES, LANES), F32),
            pltpu.SemaphoreType.DMA((2,)),
        ],
        2 * count * features * blocks * size,
    )


def run_last(given, part, mass, below, above):
    return call(
        last_kernel,
        [(given, HBM)] + [(x, VMEM) for x in (part, mass, below, above)],
        [((given.shape, BF16), HBM)],
        [VMEM(part.shape, BF16), pltpu.SemaphoreType.DMA((2,))],
        aliases={0: 0},
    )


def swap(up, down, axis):
    devices = lax.axis_size(axis)
    pairs = [(i, i + 1) for i in range(devices - 1)]
    below = lax.ppermute(up, axis, pairs)
    above = lax.ppermute(down, axis, [(j, i) for i, j in pairs])
    return below, above


def per_device(sample_rows, destination, neighbours, centroids):
    own_count, rep_count = lax.axis_size("own"), lax.axis_size("rep")
    pairs = own_count * rep_count
    count, features = sample_rows.shape
    per_pair = count // pairs
    chunks = features // LANES
    lines = count * chunks
    blocks, _, size, _ = centroids.shape
    own = centroids.reshape(blocks, size, features)
    outgoing = run_regroup(pairs, destination.reshape(1, count), sample_rows)
    left, right = swap(own[blocks - 1], own[0], "own")
    first_block = lax.axis_index("own") * blocks - 1
    ids = (neighbours // rep_count - first_block).T
    ids = ids.reshape(-1, pairs, per_pair).swapaxes(1, 2).reshape(-1, count)
    arrived = lax.all_to_all(
        outgoing.reshape(pairs, lines // pairs // 4, 4, LANES), ("own", "rep"), split_axis=0, concat_axis=0, tiled=True
    ).reshape(lines, LANES)

    ids, bias = run_prepare(ids, own)
    rows, weights1, top1, total1 = run_arrival(pairs, arrived, ids, own, bias)
    scale1, sums1, mass1, up1, down1 = run_first(rows, ids, weights1, top1, total1, left, own, right)
    below1, above1 = swap(up1, down1, "own")
    fresh, norm, inner2, top, total = run_inner(rows, ids, weights1, scale1, own)
    below_edge, below_w, top, total, shrink = run_below(rows, ids, sums1, mass1, top, total, below1)
    above_edge, above_w, above_by, below_by, inner_by, cost, up2, down2 = run_above(
        rows, ids, sums1, mass1, norm, top, total, shrink, below_w, above1
    )
    below2, above2 = swap(up2, down2, "own")
    given, part, mass2, placed = run_own(
        per_pair, rows, inner2, inner_by, below_w, below_by, above_w, above_by, below_edge, above_edge, fresh, cost
    )
    out = run_last(given, part, mass2, below2, above2)
    return out.reshape(centroids.shape), placed.reshape(count)


def solution(mesh):
    return jax.shard_map(
        per_device,
        mesh=mesh,
        in_specs=(
            P(("own", "rep"), None),
            P(("own", "rep")),
            P(("own", "rep"), None),
            P("own", "rep", None, None),
        ),
        out_specs=(P("own", "rep", None, None), P(("own", "rep"))),
        check_vma=False,
    )
```

```python
import functools
import math

import jax
import jax.numpy as jnp
from jax import lax
from jax.experimental import pallas as pl
from jax.experimental.pallas import tpu as pltpu
from jax.sharding import PartitionSpec as P

PRIOR = 1.0
LOG2E = 1.4426950408889634
LANES = 128
MASS_ROWS = 16
VMEM = pltpu.VMEM
HBM = pltpu.HBM
ANY = pl.ANY
F32 = jnp.float32
BF16 = jnp.bfloat16


def call(kernel, ins, outs, scratch=(), flops=0, limit=24, aliases=None):
    arrays = [x if space is ANY else pltpu.with_memory_space_constraint(x, space) for x, space in ins]
    made = pl.pallas_call(
        kernel,
        in_specs=[pl.BlockSpec(memory_space=space) for _, space in ins],
        out_shape=[space(*x) if space is not ANY else sds(*x) for x, space in outs],
        out_specs=[pl.BlockSpec(memory_space=space) for _, space in outs],
        scratch_shapes=list(scratch),
        input_output_aliases=aliases or {},
        compiler_params=pltpu.CompilerParams(vmem_limit_bytes=limit << 20),
        cost_estimate=pl.CostEstimate(flops=flops, bytes_accessed=1 << 20, transcendentals=0),
    )(*arrays)
    return made[0] if len(outs) == 1 else made


def sds(shape, dtype):
    return jax.ShapeDtypeStruct(shape, dtype)


def matmul(a, b, contract):
    return lax.dot_general(a, b, (contract, ((), ())), preferred_element_type=F32)


def regroup_kernel(pairs, dest_hbm, rows_hbm, out_hbm, dest_ref, rows_ref, wide, out_ref, in_sems, out_sems):
    count, features = rows_ref.shape
    per_pair = count // pairs
    chunks = features // LANES
    fetch_dest = pltpu.make_async_copy(dest_hbm, dest_ref, in_sems.at[0])
    fetch_rows = pltpu.make_async_copy(rows_hbm, rows_ref, in_sems.at[1])
    fetch_dest.start()
    fetch_rows.start()
    fetch_dest.wait()
    dest = dest_ref[...]
    place = lax.rem(dest, per_pair) * pairs + lax.div(dest, count)
    parts = 4
    step = pairs // parts
    span = step * per_pair * chunks
    rows = None
    stores = []
    for part in range(parts):
        first = part * step
        picks = []
        for slot in range(per_pair):
            ids = lax.broadcasted_iota(jnp.int32, (step, count), 0) + (slot * pairs + first)
            picks.append(jnp.where(ids == place, 1.0, 0.0).astype(BF16))
        pick = jnp.concatenate(picks, axis=0)
        if rows is None:
            fetch_rows.wait()
            rows = rows_ref[...]
        moved = matmul(pick, rows, ((1,), (0,)))
        for slot in range(per_pair):
            for f in range(chunks):
                line = (first * chunks + f) * per_pair + slot
                wide[pl.ds(line, step, stride=chunks * per_pair), :] = moved[
                    slot * step : (slot + 1) * step, f * LANES : (f + 1) * LANES
                ]
        here = pl.ds(part * span, span)
        out_ref[here, :] = wide[here, :].astype(BF16)
        store = pltpu.make_async_copy(out_ref.at[here], out_hbm.at[here], out_sems.at[part])
        store.start()
        stores.append(store)
    for store in stores:
        store.wait()


def unpack_rows(lines_ref, rows_ref, wide, pairs):
    count, features = rows_ref.shape
    per_pair = count // pairs
    chunks = features // LANES
    parts = 4
    step = pairs // parts
    span = step * per_pair * chunks
    for part in range(parts):
        here = pl.ds(part * span, span)
        wide[here, :] = lines_ref[here, :].astype(F32)
        for slot in range(per_pair):
            for f in range(chunks):
                got = wide[pl.ds(part * span + f * per_pair + slot, step, stride=chunks * per_pair), :]
                rows_ref[pl.ds(slot * pairs + part * step, step), f * LANES : (f + 1) * LANES] = got.astype(BF16)


STEP = 256


def half_scale(features):
    return 0.5 * LOG2E / math.sqrt(features)


def scored(flat, biases, slots, rows, hits):
    cross = matmul(flat, rows, ((1,), (1,)))
    size = flat.shape[0] // len(slots)
    factor = 2.0 * half_scale(flat.shape[1])
    scores = []
    for k, w in enumerate(slots):
        hit = hits[w : w + 1, :]
        scores.append(cross[k * size : (k + 1) * size] * factor + (hit - biases[k]))
    return scores


def highest(scores):
    return functools.reduce(jnp.maximum, [jnp.max(s, axis=0, keepdims=True) for s in scores])


def added(parts):
    return functools.reduce(jnp.add, [jnp.sum(p, axis=0, keepdims=True) for p in parts])


def square_biases(blocks):
    half = half_scale(blocks[0].shape[1])
    wide = [block.astype(F32) for block in blocks]
    return [jnp.sum(w * w, axis=1, keepdims=True) * half for w in wide]


def row_sums(parts):
    return [jnp.sum(p, axis=1, keepdims=True) for p in parts]


def diagonal(size):
    across = lax.broadcasted_iota(jnp.int32, (size, size), 0)
    return across == lax.broadcasted_iota(jnp.int32, (size, size), 1)


def pack_mass(masses):
    size = masses[0].shape[0]
    eye = diagonal(size)
    row = lax.broadcasted_iota(jnp.int32, (MASS_ROWS, size), 0)
    packed = jnp.zeros((MASS_ROWS, size), F32)
    for k, mass in enumerate(masses):
        line = jnp.sum(jnp.where(eye, mass, 0.0), axis=0, keepdims=True)
        high = line.astype(BF16).astype(F32)
        packed = jnp.where(row == 2 * k, high, jnp.where(row == 2 * k + 1, line - high, packed))
    return packed.astype(BF16)


def unpack_mass(packed, which):
    size = packed.shape[1]
    row = lax.broadcasted_iota(jnp.int32, packed.shape, 0)
    line = jnp.sum(jnp.where(lax.div(row, 2) == which, packed.astype(F32), 0.0), axis=0, keepdims=True)
    return jnp.sum(jnp.where(diagonal(size), line, 0.0), axis=1, keepdims=True)


def package(pkg_ref, sums, masses):
    size, features = sums[0].shape
    blocks = len(sums)
    for f in range(features // LANES):
        for k in range(blocks):
            first = (f * blocks + k) * size
            pkg_ref[first : first + size, :] = sums[k][:, f * LANES : (f + 1) * LANES].astype(BF16)
    pkg_ref[blocks * size * (features // LANES) :, :] = pack_mass(masses)


def unpack(pkg_ref, which, blocks, size):
    chunks = (pkg_ref.shape[0] - MASS_ROWS) // (blocks * size)
    firsts = [(f * blocks + which) * size for f in range(chunks)]
    sums = jnp.concatenate([pkg_ref[first : first + size, :] for first in firsts], axis=1)
    return sums.astype(F32), unpack_mass(pkg_ref[blocks * size * chunks :, :], which)


def package_lines(blocks, size, features):
    return (((blocks * size * (features // LANES) + MASS_ROWS, LANES), BF16), VMEM)


def prepare_kernel(ids_ref, own_ref, hits_ref, bias_ref):
    ids = ids_ref[...]
    hits_ref[...] = jnp.full(hits_ref.shape, -jnp.inf, F32)
    blocks, size, _ = own_ref.shape
    for w in range(blocks + 2):
        hits_ref[w : w + 1, :] = jnp.max(jnp.where(ids == w, 0.0, -jnp.inf), axis=0, keepdims=True)
    for k, bias in enumerate(square_biases([own_ref[k] for k in range(blocks)])):
        bias_ref[k * size : (k + 1) * size, :] = bias


def arrival_kernel(
    pairs, lines_ref, hits_ref, own_ref, bias_ref, rows_ref, weights_ref, top_ref, total_ref, wide
):
    blocks, size, _ = own_ref.shape
    own = [own_ref[k] for k in range(blocks)]
    biases = [bias_ref[k * size : (k + 1) * size, :] for k in range(blocks)]
    flat = jnp.concatenate(own, axis=0)
    unpack_rows(lines_ref, rows_ref, wide, pairs)
    for start in range(0, rows_ref.shape[0], STEP):
        here = slice(start, start + STEP)
        scores = scored(flat, biases, range(1, blocks + 1), rows_ref[here, :], hits_ref[:, here])
        top = highest(scores)
        top_ref[:, here] = top
        weights = [jnp.exp2(score - top) for score in scores]
        total_ref[:, here] = added(weights)
        for k in range(blocks):
            weights_ref[k * size : (k + 1) * size, here] = weights[k]


def first_kernel(
    rows_ref, hits_ref, weights_ref, top_ref, total_ref, left_ref, own_ref, right_ref,
    scale_ref, sums_ref, mass_ref, up_ref, down_ref, resp_ref,
):
    count_own, size, _ = own_ref.shape
    last = count_own + 1
    halo = [left_ref[...], right_ref[...]]
    biases = square_biases(halo)
    flat = jnp.concatenate(halo, axis=0)
    edges = (halo[0], own_ref[0], own_ref[count_own - 1], halo[1])
    mass = [0.0] * len(edges)
    for start in range(0, rows_ref.shape[0], STEP):
        here = slice(start, start + STEP)
        scores = scored(flat, biases, (0, last), rows_ref[here, :], hits_ref[:, here])
        top = jnp.maximum(highest(scores), top_ref[:, here])
        shrink = jnp.exp2(top_ref[:, here] - top)
        weights = [jnp.exp2(score - top) for score in scores]
        scale = 1.0 / (added(weights) + shrink * total_ref[:, here])
        own_scale = shrink * scale
        scale_ref[:, here] = own_scale
        resps = (
            weights[0] * scale,
            weights_ref[:size, here] * own_scale,
            weights_ref[(count_own - 1) * size :, here] * own_scale,
            weights[1] * scale,
        )
        for k, resp in enumerate(resps):
            resp_ref[k * size : (k + 1) * size, here] = resp.astype(BF16)
            mass[k] = mass[k] + resp
    mass = row_sums(mass)
    rows = rows_ref[...]
    sums = []
    for k, block in enumerate(edges):
        total = matmul(resp_ref[k * size : (k + 1) * size, :], rows, ((1,), (0,)))
        sums_ref[k] = total + PRIOR * block.astype(F32)
        sums.append(total)
        mass_ref[k * size : (k + 1) * size, :] = mass[k] + PRIOR
    package(up_ref, sums[2:], mass[2:])
    package(down_ref, sums[:2], mass[:2])


def ratio(total, tally):
    return (total * (1.0 / tally)).astype(BF16)


def inner_kernel(
    rows_ref, hits_ref, weights_ref, scale_ref, own_ref, fresh_ref, norm_ref, next_ref, top_ref, total_ref, resp_ref
):
    blocks, size, _ = own_ref.shape
    inner = blocks - 2
    count = rows_ref.shape[0]
    mass = [0.0] * inner
    for start in range(0, count, STEP):
        here = slice(start, start + STEP)
        for k in range(inner):
            there = slice(k * size, (k + 1) * size)
            resp = weights_ref[(k + 1) * size : (k + 2) * size, here] * scale_ref[:, here]
            resp_ref[there, here] = resp.astype(BF16)
            mass[k] = mass[k] + resp
    mass = row_sums(mass)
    rows = rows_ref[...]
    new = []
    for k in range(inner):
        total = matmul(resp_ref[k * size : (k + 1) * size, :], rows, ((1,), (0,)))
        new.append(ratio(total + PRIOR * own_ref[k + 1].astype(F32), mass[k] + PRIOR))
        fresh_ref[k] = new[k]
    biases = square_biases(new)
    flat = jnp.concatenate(new, axis=0)
    for start in range(0, count, STEP):
        here = slice(start, start + STEP)
        scores = scored(flat, biases, range(2, inner + 2), rows_ref[here, :], hits_ref[:, here])
        top = highest(scores)
        top_ref[:, here] = top
        safe = jnp.where(top == -jnp.inf, 0.0, top)
        weights = [jnp.exp2(score - safe) for score in scores]
        total_ref[:, here] = added(weights)
        for k in range(inner):
            next_ref[k * size : (k + 1) * size, here] = weights[k]
    eye = diagonal(LANES)
    for start in range(0, count, LANES):
        wide = rows_ref[start : start + LANES, :].astype(F32)
        norm = jnp.sum(wide * wide, axis=1, keepdims=True)
        norm_ref[:, start : start + LANES] = jnp.sum(jnp.where(eye, norm, 0.0), axis=0, keepdims=True)


def renewed(pkg_ref, sums, masses):
    new = []
    for k in range(2):
        more, tally = unpack(pkg_ref, k, 2, sums[k].shape[0])
        new.append(ratio(sums[k] + more, masses[k] + tally))
    return new


def below_kernel(
    rows_ref, hits_ref, sums_ref, mass_ref, top_ref, total_ref, below_ref,
    edge_ref, weights_ref, new_top_ref, new_total_ref, shrink_ref,
):
    size = sums_ref.shape[1]
    new = renewed(below_ref, [sums_ref[k] for k in range(2)], [mass_ref[k * size : (k + 1) * size, :] for k in range(2)])
    edge_ref[...] = new[1]
    biases = square_biases(new)
    flat = jnp.concatenate(new, axis=0)
    for start in range(0, rows_ref.shape[0], STEP):
        here = slice(start, start + STEP)
        scores = scored(flat, biases, (0, 1), rows_ref[here, :], hits_ref[:, here])
        before = top_ref[:, here]
        top = jnp.maximum(highest(scores), before)
        safe = jnp.where(top == -jnp.inf, 0.0, top)
        shrink = jnp.exp2(before - safe)
        weights = [jnp.exp2(score - safe) for score in scores]
        new_top_ref[:, here] = top
        shrink_ref[:, here] = shrink
        new_total_ref[:, here] = added(weights) + shrink * total_ref[:, here]
        for k in range(2):
            weights_ref[k * size : (k + 1) * size, here] = weights[k]


def above_kernel(
    rows_ref, hits_ref, sums_ref, mass_ref, norm_ref, top_ref, total_ref, shrink_ref, weights_ref, above_ref,
    edge_ref, outer_ref, above_scale_ref, below_scale_ref, inner_scale_ref, cost_ref, up_ref, down_ref, resp_ref,
):
    size = sums_ref.shape[1]
    last = 5
    new = renewed(
        above_ref, [sums_ref[k] for k in range(2, 4)], [mass_ref[k * size : (k + 1) * size, :] for k in range(2, 4)]
    )
    edge_ref[...] = new[0]
    biases = square_biases(new)
    flat = jnp.concatenate(new, axis=0)
    mass = [0.0, 0.0]
    half = 0.5 / math.sqrt(rows_ref.shape[1])
    for start in range(0, rows_ref.shape[0], STEP):
        here = slice(start, start + STEP)
        scores = scored(flat, biases, (last - 1, last), rows_ref[here, :], hits_ref[:, here])
        before = top_ref[:, here]
        top = jnp.maximum(highest(scores), before)
        fade = jnp.exp2(before - top)
        weights = [jnp.exp2(score - top) for score in scores]
        total = added(weights) + fade * total_ref[:, here]
        scale = 1.0 / total
        below_scale = scale * fade
        above_scale_ref[:, here] = scale
        below_scale_ref[:, here] = below_scale
        inner_scale_ref[:, here] = below_scale * shrink_ref[:, here]
        cost_ref[:, here] = norm_ref[:, here] * half - (top * (1.0 / LOG2E) + jnp.log(total))
        outer_ref[:, here] = weights[0]
        for k, resp in enumerate((weights_ref[:size, here] * below_scale, weights[1] * scale)):
            resp_ref[k * size : (k + 1) * size, here] = resp.astype(BF16)
            mass[k] = mass[k] + resp
    mass = row_sums(mass)
    rows = rows_ref[...]
    for k, pkg in enumerate((down_ref, up_ref)):
        total = matmul(resp_ref[k * size : (k + 1) * size, :], rows, ((1,), (0,)))
        package(pkg, [total], [mass[k]])


def interleave(lines_ref, out_ref, slots):
    count = lines_ref.shape[1]
    pairs = count // slots
    width = LANES * slots
    groups = pairs // LANES
    row = lax.broadcasted_iota(jnp.int32, (width, width), 0)
    lane = lax.broadcasted_iota(jnp.int32, (width, width), 1)
    pick = jnp.where(row == lax.rem(lane, slots) * LANES + lax.div(lane, slots), 1.0, 0.0).astype(BF16)
    pieces = []
    for g in range(groups):
        cuts = [lines_ref[:, s * pairs + g * LANES : s * pairs + (g + 1) * LANES] for s in range(slots)]
        left = jnp.concatenate(cuts, axis=1)
        for _ in range(3):
            piece = left.astype(BF16).astype(F32)
            pieces.append(piece)
            left = left - piece
    pieces += [jnp.zeros_like(pieces[0])] * (-len(pieces) % 16)
    moved = matmul(jnp.concatenate(pieces, axis=0).astype(BF16), pick, ((1,), (0,)))
    for g in range(groups):
        line = moved[3 * g : 3 * g + 1] + moved[3 * g + 1 : 3 * g + 2] + moved[3 * g + 2 : 3 * g + 3]
        for s in range(slots):
            out_ref[g * slots + s : g * slots + s + 1, :] = line[:, s * LANES : (s + 1) * LANES]


def own_kernel(
    slots, rows_ref, inner_ref, inner_scale_ref, below_ref, below_scale_ref, above_ref, above_scale_ref,
    below_edge_ref, above_edge_ref, fresh_ref, cost_ref,
    out_hbm, part_ref, mass_ref, placed_hbm, done_ref, resp_ref, placed_ref, sems,
):
    inner, size, _ = fresh_ref.shape
    rows = rows_ref[...]

    def summed(weights):
        mass = [0.0] * len(weights)
        for start in range(0, rows_ref.shape[0], STEP):
            here = slice(start, start + STEP)
            for k, (ref, first, by_ref) in enumerate(weights):
                resp = ref[first : first + size, here] * by_ref[:, here]
                resp_ref[k * size : (k + 1) * size, here] = resp.astype(BF16)
                mass[k] = mass[k] + resp
        sums = [
            matmul(resp_ref[k * size : (k + 1) * size, :], rows, ((1,), (0,))) for k in range(len(weights))
        ]
        return sums, row_sums(mass)

    sums, mass = summed([(inner_ref, k * size, inner_scale_ref) for k in range(inner)])
    for k in range(inner):
        done_ref[k] = ratio(sums[k] + PRIOR * fresh_ref[k].astype(F32), mass[k] + PRIOR)
    store = pltpu.make_async_copy(done_ref, out_hbm.at[pl.ds(1, inner)], sems.at[0])
    store.start()
    interleave(cost_ref, placed_ref, slots)
    place = pltpu.make_async_copy(placed_ref, placed_hbm, sems.at[1])
    place.start()
    sums, mass = summed([(below_ref, size, below_scale_ref), (above_ref, 0, above_scale_ref)])
    for k, edge_ref in enumerate((below_edge_ref, above_edge_ref)):
        part_ref[k] = sums[k] + PRIOR * edge_ref[...].astype(F32)
        mass_ref[k * size : (k + 1) * size, :] = mass[k] + PRIOR
    store.wait()
    place.wait()


def last_kernel(given_hbm, part_ref, mass_ref, below_ref, above_ref, out_hbm, done_ref, sems):
    blocks, size, _ = out_hbm.shape
    stores = []
    for e, (k, pkg) in enumerate(((0, below_ref), (blocks - 1, above_ref))):
        more, tally = unpack(pkg, 0, 1, size)
        done_ref[e] = ratio(part_ref[e] + more, mass_ref[e * size : (e + 1) * size, :] + tally)
        stores.append(pltpu.make_async_copy(done_ref.at[e], out_hbm.at[k], sems.at[e]))
        stores[-1].start()
    for store in stores:
        store.wait()


def wide_lines(lines, stride):
    return pltpu.VMEM((lines + stride + 4, LANES), F32)


def run_regroup(pairs, dest, rows):
    count, features = rows.shape
    lines = count * features // LANES
    dma = pltpu.SemaphoreType.DMA
    return call(
        functools.partial(regroup_kernel, pairs),
        [(dest, HBM), (rows, HBM)],
        [(((lines, LANES), BF16), HBM)],
        [
            VMEM((1, count), jnp.int32),
            VMEM((count, features), BF16),
            wide_lines(lines, lines // pairs),
            VMEM((lines, LANES), BF16),
            dma((2,)),
            dma((4,)),
        ],
        2 * count * features * count,
    )


def run_prepare(ids, own):
    blocks, size, _ = own.shape
    outs = [(((8, ids.shape[1]), F32), VMEM), (((blocks * size, 1), F32), VMEM)]
    return call(prepare_kernel, [(ids, VMEM), (own, VMEM)], outs)


def run_arrival(pairs, arrived, ids, own, bias):
    lines, count = arrived.shape[0], ids.shape[1]
    blocks, size, features = own.shape
    line = (((1, count), F32), VMEM)
    return call(
        functools.partial(arrival_kernel, pairs),
        [(arrived, VMEM), (ids, VMEM), (own, VMEM), (bias, VMEM)],
        [(((count, features), BF16), VMEM), (((blocks * size, count), F32), VMEM), line, line],
        [wide_lines(lines, lines // pairs)],
        2 * count * features * blocks * size,
    )


def run_first(rows, ids, weights, top, total, left, own, right):
    blocks, size, features = own.shape
    count = rows.shape[0]
    two = package_lines(2, size, features)
    return call(
        first_kernel,
        [(x, VMEM) for x in (rows, ids, weights, top, total, left, own, right)],
        [(((1, count), F32), VMEM), (((4, size, features), F32), VMEM), (((4 * size, 1), F32), VMEM), two, two],
        [VMEM((4 * size, count), BF16)],
        2 * count * features * 6 * size,
    )


def run_inner(rows, ids, weights, scale, own):
    blocks, size, features = own.shape
    count = rows.shape[0]
    inner = (blocks - 2) * size
    line = (((1, count), F32), VMEM)
    return call(
        inner_kernel,
        [(x, VMEM) for x in (rows, ids, weights, scale, own)],
        [(((blocks - 2, size, features), BF16), VMEM), line, (((inner, count), F32), VMEM), line, line],
        [VMEM((inner, count), BF16)],
        2 * count * features * 4 * size,
    )


def run_below(rows, ids, sums, mass, top, total, below):
    _, size, features = sums.shape
    count = rows.shape[0]
    line = (((1, count), F32), VMEM)
    return call(
        below_kernel,
        [(x, VMEM) for x in (rows, ids, sums, mass, top, total, below)],
        [(((size, features), BF16), VMEM), (((2 * size, count), F32), VMEM), line, line, line],
        flops=2 * count * features * 2 * size,
    )


def run_above(rows, ids, sums, mass, norm, top, total, shrink, weights, above):
    _, size, features = sums.shape
    count = rows.shape[0]
    line = (((1, count), F32), VMEM)
    one = package_lines(1, size, features)
    return call(
        above_kernel,
        [(x, VMEM) for x in (rows, ids, sums, mass, norm, top, total, shrink, weights, above)],
        [(((size, features), BF16), VMEM), (((size, count), F32), VMEM), line, line, line, line, one, one],
        [VMEM((2 * size, count), BF16)],
        2 * count * features * 4 * size,
    )


def run_own(slots, rows, inner, inner_scale, below, below_scale, above, above_scale, below_edge, above_edge, fresh, cost):
    blocks, size, features = fresh.shape[0] + 2, fresh.shape[1], fresh.shape[2]
    count = rows.shape[0]
    ins = (rows, inner, inner_scale, below, below_scale, above, above_scale, below_edge, above_edge, fresh, cost)
    return call(
        functools.partial(own_kernel, slots),
        [(x, VMEM) for x in ins],
        [
            (((blocks, size, features), BF16), HBM),
            (((2, size, features), F32), VMEM),
            (((2 * size, 1), F32), VMEM),
            (((count // LANES, LANES), F32), HBM),
        ],
        [
            VMEM((blocks - 2, size, features), BF16),
            VMEM((2 * size, count), BF16),
            VMEM((count // LANES, LANES), F32),
            pltpu.SemaphoreType.DMA((2,)),
        ],
        2 * count * features * blocks * size,
    )


def run_last(given, part, mass, below, above):
    return call(
        last_kernel,
        [(given, HBM)] + [(x, VMEM) for x in (part, mass, below, above)],
        [((given.shape, BF16), HBM)],
        [VMEM(part.shape, BF16), pltpu.SemaphoreType.DMA((2,))],
        aliases={0: 0},
    )


def swap(up, down, axis):
    devices = lax.axis_size(axis)
    pairs = [(i, i + 1) for i in range(devices - 1)]
    below = lax.ppermute(up, axis, pairs)
    above = lax.ppermute(down, axis, [(j, i) for i, j in pairs])
    return below, above


def per_device(sample_rows, destination, neighbours, centroids):
    own_count, rep_count = lax.axis_size("own"), lax.axis_size("rep")
    pairs = own_count * rep_count
    count, features = sample_rows.shape
    per_pair = count // pairs
    chunks = features // LANES
    lines = count * chunks
    blocks, _, size, _ = centroids.shape
    own = centroids.reshape(blocks, size, features)
    outgoing = run_regroup(pairs, destination.reshape(1, count), sample_rows)
    left, right = swap(own[blocks - 1], own[0], "own")
    first_block = lax.axis_index("own") * blocks - 1
    ids = (neighbours // rep_count - first_block).T
    ids = ids.reshape(-1, pairs, per_pair).swapaxes(1, 2).reshape(-1, count)
    arrived = lax.all_to_all(
        outgoing.reshape(pairs, lines // pairs // 4, 4, LANES), ("own", "rep"), split_axis=0, concat_axis=0, tiled=True
    ).reshape(lines, LANES)

    ids, bias = run_prepare(ids, own)
    rows, weights1, top1, total1 = run_arrival(pairs, arrived, ids, own, bias)
    scale1, sums1, mass1, up1, down1 = run_first(rows, ids, weights1, top1, total1, left, own, right)
    below1, above1 = swap(up1, down1, "own")
    fresh, norm, inner2, top, total = run_inner(rows, ids, weights1, scale1, own)
    below_edge, below_w, top, total, shrink = run_below(rows, ids, sums1, mass1, top, total, below1)
    above_edge, above_w, above_by, below_by, inner_by, cost, up2, down2 = run_above(
        rows, ids, sums1, mass1, norm, top, total, shrink, below_w, above1
    )
    below2, above2 = swap(up2, down2, "own")
    given, part, mass2, placed = run_own(
        per_pair, rows, inner2, inner_by, below_w, below_by, above_w, above_by, below_edge, above_edge, fresh, cost
    )
    out = run_last(given, part, mass2, below2, above2)
    return out.reshape(centroids.shape), placed.reshape(count)


def solution(mesh):
    return jax.shard_map(
        per_device,
        mesh=mesh,
        in_specs=(
            P(("own", "rep"), None),
            P(("own", "rep")),
            P(("own", "rep"), None),
            P("own", "rep", None, None),
        ),
        out_specs=(P("own", "rep", None, None), P(("own", "rep"))),
        check_vma=False,
    )
```
